512 devices in a mesh: dp: 8 (over z_hi, y), rows: 64 (over x, z_lo, core).
Axes of the slice: x: 4, y: 4, z: 16 (z_hi: 2, z_lo: 8; z = z_hi * 8 + z_lo), core: 2. Of those that a mesh axis runs over, the one named last changes fastest.
Arguments:
- fake: bfloat16 [8, 3, 256, 256], P('dp', None, 'rows'), may hold values from -1 to 1
- real: bfloat16 [8, 3, 256, 256], P('dp', None, 'rows'), may hold values from -1 to 1
- vgg_first: bfloat16 [64, 3, 3, 3], replicated, may hold values from -1.25 to 1.25
- vgg_second: bfloat16 [64, 64, 3, 3], replicated, may hold values from -0.25 to 0.25
- lpips_weights: float32 [64], replicated, may hold values from 0.5 to 2
- critic_conv: bfloat16 [64, 3, 4, 4], replicated, may hold values from -0.875 to 0.875
- critic_head: float32 [64], replicated, may hold values from -0.75 to 0.75
Outputs:
- grad_fake: float32 [8, 3, 256, 256], P('dp', None, 'rows')
- conv_grad: float32 [64, 3, 4, 4], replicated
- head_grad: float32 [64], replicated
The draws below stay inside these ranges and needn't reach their ends.
All inputs are finite; a program needn't handle non-finite values.
Results may differ from the reference program's by a relative error of at most 0.0053.
Values may be sent and summed in bfloat16 or wider, within the bound.
No kernel may reach another device: no remote copies, remote signals or barrier semaphores. Data moves between devices by JAX's collectives and lax.ppermute only.
A program may use at most 64 MiB of HBM per device.

```python
import jax
import jax.numpy as jnp
from jax import lax

VGG_CH = 64
NDF = 64
WIDTH = 256
HEIGHT = 256
IMAGES = 8


def shard_levels(stream_key, dims, cuts, low, largest):
    level, own = 1.0, jax.random.fold_in(stream_key, 6)
    for position, blocks in cuts:
        steps = jnp.exp(jax.random.uniform(jax.random.fold_in(own, position), (blocks,), jnp.float32, low / len(cuts), largest / len(cuts)))
        level = level * jnp.repeat(steps, dims[position] // blocks).reshape([-1 if axis == position else 1 for axis in range(len(dims))])
    return level


def scatter_about(rng, extent, scale, limit, kind=jnp.bfloat16):
    values = scale * jax.random.normal(rng, extent, jnp.float32)
    return jnp.clip(values, min=-limit, max=limit).astype(kind)


def setup_inputs(seed: int = 0) -> dict:
    arg_keys = jax.random.split(jax.random.key(seed), 8)
    fake = jnp.clip(jax.random.uniform(arg_keys[0], (IMAGES, 3, HEIGHT, WIDTH), jnp.float32, -1.0, 1.0) * shard_levels(arg_keys[0], (IMAGES, 3, HEIGHT, WIDTH), ((0, 8), (2, 64)), -0.4, 0.0), -1.0, 1.0).astype(jnp.bfloat16)
    real = jnp.clip(jax.random.uniform(arg_keys[1], (IMAGES, 3, HEIGHT, WIDTH), jnp.float32, -1.0, 1.0) * shard_levels(arg_keys[1], (IMAGES, 3, HEIGHT, WIDTH), ((0, 8), (2, 64)), -0.4, 0.0), -1.0, 1.0).astype(jnp.bfloat16)
    vgg_first = scatter_about(arg_keys[2], (VGG_CH, 3, 3, 3), 27 ** -0.5, 1.25)
    vgg_second = scatter_about(arg_keys[3], (VGG_CH, VGG_CH, 3, 3), (9 * VGG_CH) ** -0.5, 0.25)
    lpips_weights = jnp.clip(jax.random.uniform(arg_keys[4], (VGG_CH,), jnp.float32, 0.5, 2.0), 0.5, 2.0)
    critic_conv = scatter_about(arg_keys[5], (NDF, 3, 4, 4), 48 ** -0.5, 0.875)
    critic_head = scatter_about(arg_keys[6], (NDF,), NDF ** -0.5, 0.75, jnp.float32)
    return dict(fake=fake, real=real, vgg_first=vgg_first, vgg_second=vgg_second, lpips_weights=lpips_weights, critic_conv=critic_conv, critic_head=critic_head)


LPIPS_SHIFT = (-0.03, -0.088, -0.188)
LPIPS_SCALE = (0.458, 0.448, 0.45)
SOFTNESS = 0.04

def smooth_relu(value):
    return 0.5 * (value + jnp.sqrt(value * value + SOFTNESS))

def smooth_grad(value):
    return 0.5 * (1.0 + value / jnp.sqrt(value * value + SOFTNESS))

def leaky_value(value):
    return 0.6 * value + 0.4 * jnp.sqrt(value * value + SOFTNESS)

def leaky_slope(value):
    return 0.6 + 0.4 * value / jnp.sqrt(value * value + SOFTNESS)

def padded_all(tensor):
    return jnp.pad(tensor, ((0, 0), (0, 0), (1, 1), (1, 1)))

def forward_taps(inputs, weight):
    rows_out = inputs.shape[2] - 2
    cols_out = inputs.shape[3] - 2
    total = jnp.zeros((inputs.shape[0], weight.shape[0], rows_out, cols_out), jnp.float32)
    for row_tap in range(3):
        for col_tap in range(3):
            window = inputs[:, :, row_tap:row_tap + rows_out, col_tap:col_tap + cols_out]
            total = total + jnp.einsum('oi,birc->borc', weight[:, :, row_tap, col_tap].astype(jnp.float32), window.astype(jnp.float32))
    return total

def backward_taps(inputs, weight):
    rows_out = inputs.shape[2] - 2
    cols_out = inputs.shape[3] - 2
    total = jnp.zeros((inputs.shape[0], weight.shape[1], rows_out, cols_out), jnp.float32)
    for row_tap in range(3):
        for col_tap in range(3):
            window = inputs[:, :, 2 - row_tap:2 - row_tap + rows_out, 2 - col_tap:2 - col_tap + cols_out]
            total = total + jnp.einsum('oi,borc->birc', weight[:, :, row_tap, col_tap].astype(jnp.float32), window.astype(jnp.float32))
    return total

def critic_forward(inputs, weight):
    outputs = (inputs.shape[2] - 2) // 2
    half = (inputs.shape[3] - 2) // 2
    total = jnp.zeros((inputs.shape[0], weight.shape[0], outputs, half), jnp.float32)
    for row_tap in range(4):
        for col_tap in range(4):
            window = inputs[:, :, row_tap:row_tap + 2 * outputs - 1:2, col_tap:col_tap + 2 * half - 1:2]
            total = total + jnp.einsum('oc,bcrj->borj', weight[:, :, row_tap, col_tap].astype(jnp.float32), window.astype(jnp.float32))
    return total

def critic_backward(grads, weight):
    outputs = grads.shape[2]
    half = grads.shape[3]
    total = jnp.zeros((grads.shape[0], weight.shape[1], 2 * outputs + 2, 2 * half + 2), jnp.float32)
    for row_tap in range(4):
        for col_tap in range(4):
            term = jnp.einsum('oc,borj->bcrj', weight[:, :, row_tap, col_tap].astype(jnp.float32), grads.astype(jnp.float32))
            total = total.at[:, :, row_tap:row_tap + 2 * outputs - 1:2, col_tap:col_tap + 2 * half - 1:2].add(term)
    return total

def critic_weights(signal, inputs):
    outputs = signal.shape[2]
    half = signal.shape[3]
    rows_list = []
    for row_tap in range(4):
        cols_list = []
        for col_tap in range(4):
            window = inputs[:, :, row_tap:row_tap + 2 * outputs - 1:2, col_tap:col_tap + 2 * half - 1:2].astype(jnp.float32)
            cols_list.append(jnp.einsum('borj,bcrj->oc', signal, window, precision=lax.Precision.HIGHEST))
        rows_list.append(jnp.stack(cols_list, axis=-1))
    return jnp.stack(rows_list, axis=-2)

def lpips_gradient(features, weights):
    norm = jnp.sqrt(lax.optimization_barrier(jnp.sum(features * features, axis=1)) + 1e-06)
    unit = features / norm[:, None]
    direction = 2.0 * weights[:, None, None] * (unit[0] - unit[1])
    inner = lax.optimization_barrier(jnp.sum(direction * unit[0], axis=0))
    return ((direction - unit[0] * inner[None]) / norm[0][None])[None]

def reference(fake, real, vgg_first, vgg_second, lpips_weights, critic_conv, critic_head):
    total_patches = fake.shape[0] * (fake.shape[2] // 2) * (fake.shape[3] // 2)
    shift = jnp.array(LPIPS_SHIFT, jnp.float32)[:, None, None]
    scale = jnp.array(LPIPS_SCALE, jnp.float32)[:, None, None]

    def per_image(pair):
        fake_one, real_one = pair
        height = fake_one.shape[1]
        width = fake_one.shape[2]
        images = jnp.stack([fake_one, real_one])
        scaled = ((images.astype(jnp.float32) - shift) / scale).astype(jnp.bfloat16)
        pre_first = forward_taps(padded_all(scaled), vgg_first)
        act_first = smooth_relu(pre_first).astype(jnp.bfloat16)
        pre_second = forward_taps(padded_all(act_first), vgg_second)
        grad_feature = lpips_gradient(smooth_relu(pre_second), lpips_weights)
        grad_second = (grad_feature * smooth_grad(pre_second[0:1])).astype(jnp.bfloat16)
        grad_act = backward_taps(padded_all(grad_second), vgg_second)
        grad_first = (grad_act * smooth_grad(pre_first[0:1])).astype(jnp.bfloat16)
        grad_scaled = backward_taps(padded_all(grad_first), vgg_first)
        padded = padded_all(images)
        pre_critic = critic_forward(padded, critic_conv)
        slope = leaky_slope(pre_critic)
        hidden = leaky_value(pre_critic)
        logits = jnp.einsum('o,borj->brj', critic_head, hidden, precision=lax.Precision.HIGHEST)
        gen_signal = (-critic_head[None, :, None, None] * slope[0:1]).astype(jnp.bfloat16)
        grad_gan = critic_backward(gen_signal, critic_conv)[0, :, 1:height + 1, 1:width + 1]
        grad_image = grad_scaled[0] / scale + grad_gan
        logit_grad = jnp.stack([jnp.where(logits[0] > -1.0, 1.0, 0.0), jnp.where(logits[1] < 1.0, -1.0, 0.0)]) / total_patches
        head_part = jnp.einsum('brj,borj->o', logit_grad, hidden, precision=lax.Precision.HIGHEST)
        critic_signal = critic_head[None, :, None, None] * logit_grad[:, None] * slope
        conv_part = critic_weights(critic_signal, padded)
        return (grad_image, conv_part, head_part)
    grad_fake, conv_parts, head_parts = lax.map(per_image, (fake, real))
    return (grad_fake, lax.optimization_barrier(jnp.sum(conv_parts, axis=0)), lax.optimization_barrier(jnp.sum(head_parts, axis=0)))
```

```python
import functools

import jax
import jax.numpy as jnp
from jax import lax
from jax.experimental import pallas as pl
from jax.experimental.pallas import tpu as pltpu
from jax.sharding import Mesh, PartitionSpec as P

LPIPS_SHIFT = (-0.03, -0.088, -0.188)
LPIPS_SCALE = (0.458, 0.448, 0.45)
SOFTNESS = 0.04
ROWS = ("x", "zl", "c")
DP = ("zh", "y")
PLANE = ("y", "x", "c")
COLUMN = ("zh", "zl")
F32 = jnp.float32
BF16 = jnp.bfloat16
VMEM = pl.BlockSpec(memory_space=pltpu.VMEM)
SMEM = pl.BlockSpec(memory_space=pltpu.SMEM)
TN = (((0,), (0,)), ((), ()))
NT = (((1,), (1,)), ((), ()))


def iota(shape, dim):
    return lax.broadcasted_iota(jnp.int32, shape, dim)


def dot(lhs, rhs):
    return jnp.dot(lhs, rhs, preferred_element_type=F32)


def split(value):
    high = value.astype(BF16)
    return high, (value - high.astype(F32)).astype(BF16)


def tap_index(m):
    return m >> 4, (m >> 2) & 3, m & 3


def block_index(k):
    tap = (k >= 48).astype(jnp.int32) + (k >= 96).astype(jnp.int32) + (k >= 144).astype(jnp.int32)
    rest = k - 48 * tap
    return tap, rest >> 4, rest & 15


def prepare_kernel(first_ref, second_ref, critic_ref, spread_ref, critic_fwd_ref, critic_bwd_ref,
                   first_fwd_ref, first_bwd_ref, second_fwd_ref, second_bwd_ref):
    column = iota((256, 512), 0)
    place = iota((256, 512), 1)
    spread_ref[...] = (column == 2 * (place & 127) + (place >> 7) - 1).astype(F32).astype(BF16)

    def expand(weight, width, first_row):
        channel, row_tap, col_tap = tap_index(iota((48, width), 0))
        block_tap, block_channel, block_row = block_index(iota((48, width), 1))
        chosen = (channel == block_channel) & (col_tap == block_tap) & (block_row == first_row + row_tap)
        return lax.dot_general(
            weight, chosen.astype(F32).astype(BF16), TN, preferred_element_type=F32
        ).astype(BF16)

    critic = critic_ref[...]
    first = first_ref[...]
    for patch in range(4):
        critic_fwd_ref[64 * patch : 64 * patch + 64, :] = expand(critic, 192, 1 + 2 * patch)
    for row in range(10):
        first_fwd_ref[64 * row : 64 * row + 64, :] = expand(first, 144, row)

    def gather(weight, shift):
        row = iota((64, 48), 0)
        channel, row_tap, col_tap = tap_index(iota((64, 48), 1))
        inner = row & 15
        chosen = (row >> 4 == col_tap) & (inner >> 2 == channel) & ((inner & 3) + shift == row_tap)
        return dot(chosen.astype(F32).astype(BF16), weight).astype(BF16)

    critic_bwd_ref[...] = jnp.concatenate([gather(critic, 3 - 2 * patch) for patch in range(4)], axis=1)
    first_bwd_ref[...] = jnp.concatenate([gather(first, 2 - row)[:48] for row in range(6)], axis=1)
    for row_tap in range(3):
        second_fwd_ref[64 * row_tap : 64 * row_tap + 64, :] = jnp.concatenate(
            [second_ref[row_tap, col_tap] for col_tap in range(3)], axis=1
        )
        second_bwd_ref[64 * row_tap : 64 * row_tap + 64, :] = jnp.concatenate(
            [second_ref[row_tap, col_tap].astype(F32).T.astype(BF16) for col_tap in range(3)], axis=1
        )


def prepare(first, second, critic):
    shapes = [(256, 512), (256, 192), (64, 256), (640, 144), (48, 384), (192, 192), (192, 192)]
    return pl.pallas_call(
        prepare_kernel,
        out_shape=[jax.ShapeDtypeStruct(shape, BF16) for shape in shapes],
        in_specs=[VMEM] * 3,
        out_specs=[VMEM] * len(shapes),
        name="prepare",
    )(first, second, critic)


def critic_kernel(row_ref, image_ref, spread_ref, weight_ref, head_ref, sums_ref, signal_ref):
    first_patch = row_ref[0] // 2 - 1
    taps = dot(image_ref[...], spread_ref[...]).astype(BF16)
    windows = jnp.concatenate(
        [
            jnp.concatenate([taps[48 * image : 48 * image + 48, 128 * tap : 128 * tap + 128] for tap in range(4)], axis=0)
            for image in range(2)
        ],
        axis=1,
    )
    pre = dot(weight_ref[...], windows)
    head = head_ref[...]
    square = pre * pre + SOFTNESS
    inverse = lax.rsqrt(square)
    hidden = 0.6 * pre + 0.4 * (square * inverse)
    slope = 0.6 + 0.4 * (pre * inverse)
    for patch in range(4):
        valid = ((first_patch + patch >= 0) & (first_patch + patch < 128)).astype(F32)
        signal_ref[64 * patch : 64 * patch + 64, :] = (
            slope[64 * patch : 64 * patch + 64, :128] * (head * -valid)
        ).astype(BF16)
    lane = iota((1, 256), 1)
    signals = []
    hiddens = []
    for patch in (1, 2):
        part = hidden[64 * patch : 64 * patch + 64]
        logit = jnp.sum(head * part, axis=0, keepdims=True)
        sign = jnp.where(
            lane < 128, jnp.where(logit > -1.0, 1.0, 0.0), jnp.where(logit < 1.0, -1.0, 0.0)
        )
        signals.append(slope[64 * patch : 64 * patch + 64] * head * sign)
        hiddens.append(part * sign)
    signal = jnp.concatenate(signals, axis=0)
    high, low = split(signal)
    grads = lax.dot_general(windows, high, NT, preferred_element_type=F32) + lax.dot_general(
        windows, low, NT, preferred_element_type=F32
    )
    rows = []
    for block in range(12):
        here = grads[16 * block : 16 * block + 16]
        rows.append(here[3:7, :64] + here[5:9, 64:])
    sums_ref[0:24, :] = 128.0 * jnp.concatenate(
        [jnp.concatenate(rows[:6], axis=0), jnp.concatenate(rows[6:], axis=0)], axis=1
    )
    total = hiddens[0] + hiddens[1]
    ones = jnp.ones((8, 256), BF16)
    high, low = split(total)
    low, rest = split(total - high.astype(F32))
    head_sum = (
        lax.dot_general(ones, high, NT, preferred_element_type=F32)
        + lax.dot_general(ones, low, NT, preferred_element_type=F32)
        + lax.dot_general(ones, rest, NT, preferred_element_type=F32)
    )
    sums_ref[24:32, :] = jnp.concatenate([head_sum, jnp.zeros((8, 64), F32)], axis=1)


def critic(first_row, image, spread, weight, head):
    return pl.pallas_call(
        critic_kernel,
        out_shape=[jax.ShapeDtypeStruct((32, 128), F32), jax.ShapeDtypeStruct((256, 128), BF16)],
        in_specs=[SMEM] + [VMEM] * 4,
        out_specs=[VMEM] * 2,
        name="critic",
    )(first_row, image, spread, weight, head)


def shifted(value, step):
    if step == 0:
        return value
    zero = jnp.zeros(value.shape[:1] + (1,), value.dtype)
    parts = []
    for start in range(0, value.shape[1], 256):
        here = value[:, start : start + 256]
        if step > 0:
            parts.append(jnp.concatenate([here[:, 1:], zero], axis=1))
        else:
            parts.append(jnp.concatenate([zero, here[:, :-1]], axis=1))
    return parts[0] if len(parts) == 1 else jnp.concatenate(parts, axis=1)


def feature_kernel(row_ref, image_ref, signal_ref, lpips_ref, spread_ref, critic_bwd_ref, first_fwd_ref,
                   first_bwd_ref, second_fwd_ref, second_bwd_ref, out_ref, slope_ref, pre_ref, act_ref):
    first_row = row_ref[0]

    def valid(row):
        return ((first_row + row >= 0) & (first_row + row < 256)).astype(F32)

    line = iota((16, 256), 0) + (first_row - 4)
    inside = ((line >= 0) & (line < 256)).astype(F32)
    images = []
    for image in range(2):
        parts = []
        for channel in range(3):
            start = 48 * image + 16 * channel
            here = image_ref[start : start + 16, :].astype(F32)
            parts.append((here - LPIPS_SHIFT[channel]) / LPIPS_SCALE[channel] * inside)
        images.append(jnp.concatenate(parts, axis=0))
    scaled = jnp.concatenate(images, axis=1)
    windows = jnp.concatenate([shifted(scaled, step).astype(BF16) for step in (-1, 0, 1)], axis=0)
    pre_ref[...] = dot(first_fwd_ref[...], windows)
    for row in range(10):
        value = pre_ref[64 * row : 64 * row + 64, :]
        square = value * value + SOFTNESS
        inverse = lax.rsqrt(square)
        if 2 <= row < 8:
            slope_ref[64 * row - 128 : 64 * row - 64, :] = 0.5 + 0.5 * (value * inverse)[:, :256]
        act = (value + square * inverse) * (0.5 * valid(row - 3))
        stack = jnp.concatenate([shifted(act, step).astype(BF16) for step in (-1, 0, 1)], axis=0)
        product = dot(second_fwd_ref[...], stack)
        for row_tap in range(3):
            target = row - row_tap
            if 0 <= target < 8:
                part = product[64 * row_tap : 64 * row_tap + 64]
                if row_tap == 0:
                    act_ref[64 * target : 64 * target + 64, :] = part
                else:
                    act_ref[64 * target : 64 * target + 64, :] += part
    weights = lpips_ref[...]
    acts = [None] * 6
    for row in range(8):
        value = act_ref[64 * row : 64 * row + 64, :]
        square = value * value + SOFTNESS
        inverse = lax.rsqrt(square)
        feature = 0.5 * (value + square * inverse)
        power = jnp.sum(feature * feature, axis=0, keepdims=True) + 1e-6
        norm = lax.rsqrt(power)
        unit = feature * norm
        unit_fake = unit[:, :256]
        direction = weights * (unit_fake - unit[:, 256:])
        inner = jnp.sum(direction * unit_fake, axis=0, keepdims=True)
        slope = 0.5 + 0.5 * (value[:, :256] * inverse[:, :256])
        grad = (direction - unit_fake * inner) * slope * (norm[:, :256] * (2.0 * valid(row - 2)))
        stack = jnp.concatenate([shifted(grad, step).astype(BF16) for step in (1, 0, -1)], axis=0)
        product = dot(second_bwd_ref[...], stack)
        for row_tap in range(3):
            target = row - 2 + row_tap
            if 0 <= target < 6:
                part = product[64 * row_tap : 64 * row_tap + 64]
                acts[target] = part if acts[target] is None else acts[target] + part
    grads = jnp.concatenate(
        [
            (acts[row] * slope_ref[64 * row : 64 * row + 64, :] * valid(row - 1)).astype(BF16)
            for row in range(6)
        ],
        axis=0,
    )
    product = dot(first_bwd_ref[...], grads)
    image_grad = shifted(product[0:16], 1) + product[16:32] + shifted(product[32:48], -1)
    product = dot(critic_bwd_ref[...], signal_ref[...])
    taps = jnp.concatenate([product[16 * tap : 16 * tap + 16] for tap in range(4)], axis=1)
    high, low = split(taps)
    critic_grad = lax.dot_general(high, spread_ref[...], NT, preferred_element_type=F32) + lax.dot_general(
        low, spread_ref[...], NT, preferred_element_type=F32
    )
    for channel in range(3):
        out_ref[channel] = (
            image_grad[4 * channel : 4 * channel + 4] / LPIPS_SCALE[channel]
            + critic_grad[4 * channel : 4 * channel + 4]
        )


def features(first_row, image, signal, lpips, spread, critic_bwd, first_fwd, first_bwd, second_fwd, second_bwd):
    return pl.pallas_call(
        feature_kernel,
        out_shape=jax.ShapeDtypeStruct((3, 4, 256), F32),
        in_specs=[SMEM] + [VMEM] * 9,
        out_specs=VMEM,
        scratch_shapes=[
            pltpu.VMEM((384, 256), F32),
            pltpu.VMEM((640, 512), F32),
            pltpu.VMEM((512, 512), F32),
        ],
        compiler_params=pltpu.CompilerParams(vmem_limit_bytes=32 * 1024 * 1024),
        cost_estimate=pl.CostEstimate(flops=1_000_000_000, bytes_accessed=1_000_000, transcendentals=1_000_000),
        name="features",
    )(first_row, image, signal, lpips, spread, critic_bwd, first_fwd, first_bwd, second_fwd, second_bwd)


def weight_rows(weight):
    moved = jnp.transpose(weight, (1, 2, 3, 0))
    taps = moved.shape[1]
    return jnp.pad(moved, ((0, 0), (0, 4 - taps), (0, 4 - taps), (0, 0))).reshape(48, 64)


def exchange_sum(value, axes):
    peers = lax.axis_size(axes)
    copies = jnp.broadcast_to(value[None], (peers,) + value.shape)
    return jnp.sum(lax.all_to_all(copies, axes, 0, 0).astype(F32), axis=0)


def shards(fake, real, vgg_first, vgg_second, lpips_weights, critic_conv, critic_head):
    count = lax.axis_size(ROWS)
    first_row = (lax.axis_index(ROWS) * 4).astype(jnp.int32)[None]
    images = jnp.concatenate([fake, real], axis=0)
    far_pairs = [(2 * k + 1, 2 * k + 2) for k in range(count // 2 - 1)]
    far = lax.ppermute(images, ROWS, far_pairs + [(b, a) for a, b in far_pairs])
    near = lax.ppermute(images, "c", [(0, 1), (1, 0)])
    spread, critic_fwd, critic_bwd, first_fwd, first_bwd, second_fwd, second_bwd = prepare(
        weight_rows(vgg_first), jnp.transpose(vgg_second, (2, 3, 0, 1)), weight_rows(critic_conv)
    )
    lower = lax.axis_index("c") == 0
    image = jnp.concatenate(
        [jnp.where(lower, far, near), images, jnp.where(lower, near, far), jnp.zeros_like(images)], axis=2
    ).reshape(96, 256)
    sums, signal = critic(first_row, image, spread, critic_fwd, critic_head[:, None])
    plane = exchange_sum(sums.astype(jnp.float16), PLANE)
    total = exchange_sum((plane * (1.0 / 32.0)).astype(jnp.float16), COLUMN)
    grad_image = features(
        first_row, image, signal, lpips_weights[:, None], spread, critic_bwd, first_fwd, first_bwd, second_fwd,
        second_bwd,
    )
    patches = 8 * 128 * 128
    conv = jnp.concatenate([total[:24, :64], total[:24, 64:]], axis=0) * (32.0 / 128.0 / patches)
    conv_grad = jnp.transpose(conv.reshape(4, 3, 4, 64), (3, 1, 2, 0))
    head_grad = (total[24, :64] + total[24, 64:]) * (32.0 / patches)
    return grad_image[None], conv_grad, head_grad


def solution(mesh):
    wide = Mesh(mesh.devices.reshape(2, 4, 4, 8, 2), ("zh", "y", "x", "zl", "c"))
    return jax.shard_map(
        shards,
        mesh=wide,
        in_specs=(P(DP, None, ROWS, None), P(DP, None, ROWS, None), P(), P(), P(), P(), P()),
        out_specs=(P(DP, None, ROWS, None), P(), P()),
        check_vma=False,
    )
```

```python
import functools

import jax
import jax.numpy as jnp
from jax import lax
from jax.experimental import pallas as pl
from jax.experimental.pallas import tpu as pltpu
from jax.sharding import Mesh, PartitionSpec as P

LPIPS_SHIFT = (-0.03, -0.088, -0.188)
LPIPS_SCALE = (0.458, 0.448, 0.45)
SOFTNESS = 0.04
ROWS = ("x", "zl", "c")
DP = ("zh", "y")
PLANE = ("y", "x", "c")
COLUMN = ("zh", "zl")
F32 = jnp.float32
BF16 = jnp.bfloat16
VMEM = pl.BlockSpec(memory_space=pltpu.VMEM)
SMEM = pl.BlockSpec(memory_space=pltpu.SMEM)
TN = (((0,), (0,)), ((), ()))
NT = (((1,), (1,)), ((), ()))
SMALL = pltpu.CompilerParams(vmem_limit_bytes=8 * 1024 * 1024)


def iota(shape, dim):
    return lax.broadcasted_iota(jnp.int32, shape, dim)


def dot(lhs, rhs):
    return jnp.dot(lhs, rhs, preferred_element_type=F32)


def split(value):
    high = value.astype(BF16)
    return high, (value - high.astype(F32)).astype(BF16)


def tap_index(m):
    return m >> 4, (m >> 2) & 3, m & 3


def block_index(k):
    tap = (k >= 48).astype(jnp.int32) + (k >= 96).astype(jnp.int32) + (k >= 144).astype(jnp.int32)
    rest = k - 48 * tap
    return tap, rest >> 4, rest & 15


def place_rows(previous_ref, image_ref, next_ref, image, channel):
    parts = [ref[image, channel].astype(F32) for ref in (previous_ref, image_ref, next_ref)]
    return jnp.concatenate(parts + [jnp.zeros_like(parts[0])], axis=0)


def expand(weight, width, first_row):
    channel, row_tap, col_tap = tap_index(iota((48, width), 0))
    block_tap, block_channel, block_row = block_index(iota((48, width), 1))
    chosen = (channel == block_channel) & (col_tap == block_tap) & (block_row == first_row + row_tap)
    return lax.dot_general(
        weight, chosen.astype(F32).astype(BF16), TN, preferred_element_type=F32
    ).astype(BF16)


def critic_weights_kernel(critic_ref, head_ref, spread_ref, fwd_ref, column_ref):
    column = iota((256, 512), 0)
    place = iota((256, 512), 1)
    spread_ref[...] = (column == 2 * (place & 127) + (place >> 7) - 1).astype(F32).astype(BF16)
    critic = critic_ref[...]
    for patch in range(4):
        fwd_ref[64 * patch : 64 * patch + 64, :] = expand(critic, 192, 1 + 2 * patch)
    diagonal = iota((64, 64), 0) == iota((64, 64), 1)
    column_ref[...] = jnp.sum(jnp.where(diagonal, head_ref[...], 0.0), axis=1, keepdims=True)


def critic_weights(critic, head):
    return pl.pallas_call(
        critic_weights_kernel,
        out_shape=[
            jax.ShapeDtypeStruct((256, 512), BF16),
            jax.ShapeDtypeStruct((256, 192), BF16),
            jax.ShapeDtypeStruct((64, 1), F32),
        ],
        in_specs=[VMEM] * 2,
        out_specs=[VMEM] * 3,
        compiler_params=SMALL,
        name="critic_weights",
    )(critic, head)


def feature_weights_kernel(first_ref, second_ref, critic_ref, critic_bwd_ref, first_fwd_ref, first_bwd_ref,
                           second_fwd_ref, second_bwd_ref):
    critic = critic_ref[...]
    first = first_ref[...]
    for row in range(10):
        first_fwd_ref[64 * row : 64 * row + 64, :] = expand(first, 144, row)

    def gather(weight, shift):
        row = iota((64, 48), 0)
        channel, row_tap, col_tap = tap_index(iota((64, 48), 1))
        inner = row & 15
        chosen = (row >> 4 == col_tap) & (inner >> 2 == channel) & ((inner & 3) + shift == row_tap)
        return dot(chosen.astype(F32).astype(BF16), weight).astype(BF16)

    critic_bwd_ref[...] = jnp.concatenate([gather(critic, 3 - 2 * patch) for patch in range(4)], axis=1)
    first_bwd_ref[...] = jnp.concatenate([gather(first, 2 - row)[:48] for row in range(6)], axis=1)
    for row_tap in range(3):
        second_fwd_ref[64 * row_tap : 64 * row_tap + 64, :] = jnp.concatenate(
            [second_ref[row_tap, col_tap] for col_tap in range(3)], axis=1
        )
        second_bwd_ref[64 * row_tap : 64 * row_tap + 64, :] = jnp.concatenate(
            [second_ref[row_tap, col_tap].astype(F32).T.astype(BF16) for col_tap in range(3)], axis=1
        )


def feature_weights(first, second, critic):
    shapes = [(64, 256), (640, 144), (48, 384), (192, 192), (192, 192)]
    return pl.pallas_call(
        feature_weights_kernel,
        out_shape=[jax.ShapeDtypeStruct(shape, BF16) for shape in shapes],
        in_specs=[VMEM] * 3,
        out_specs=[VMEM] * len(shapes),
        compiler_params=SMALL,
        cost_estimate=pl.CostEstimate(flops=100_000_000, bytes_accessed=1_000_000, transcendentals=0),
        name="feature_weights",
    )(first, second, critic)


def stack_taps(taps, image):
    return jnp.concatenate(
        [taps[48 * image : 48 * image + 48, 128 * tap : 128 * tap + 128] for tap in range(4)], axis=0
    )


def critic_kernel(row_ref, previous_ref, image_ref, next_ref, spread_ref, weight_ref, head_ref, sums_ref):
    index = row_ref[0] // 4
    takes = (((index & 15) == 0) & (index > 0)).astype(F32)
    keeps = 1.0 - (((index & 15) == 15) & (index < 63)).astype(F32)
    image = jnp.concatenate(
        [
            place_rows(previous_ref, image_ref, next_ref, image, channel)
            for image in range(2)
            for channel in range(3)
        ],
        axis=0,
    ).astype(BF16)
    taps = dot(image, spread_ref[...]).astype(BF16)
    windows = jnp.concatenate([stack_taps(taps, 0), stack_taps(taps, 1)], axis=1)
    pre = dot(weight_ref[0:192, :], windows)
    head = head_ref[...]
    square = pre * pre + SOFTNESS
    inverse = lax.rsqrt(square)
    hidden = 0.6 * pre + 0.4 * (square * inverse)
    slope = 0.6 + 0.4 * (pre * inverse)
    lane = iota((1, 256), 1)
    signals = []
    total = None
    for patch, share in enumerate((takes, 1.0, keeps)):
        part = hidden[64 * patch : 64 * patch + 64]
        logit = jnp.sum(head * part, axis=0, keepdims=True)
        sign = jnp.where(
            lane < 128, jnp.where(logit > -1.0, 1.0, 0.0), jnp.where(logit < 1.0, -1.0, 0.0)
        ) * share
        signals.append(slope[64 * patch : 64 * patch + 64] * head * sign)
        total = part * sign if total is None else total + part * sign
    high, low = split(jnp.concatenate(signals + [total], axis=0))
    windows = jnp.concatenate([windows, jnp.ones((16, 256), BF16)], axis=0)
    grads = lax.dot_general(windows, high, NT, preferred_element_type=F32) + lax.dot_general(
        windows, low, NT, preferred_element_type=F32
    )
    rows = []
    for block in range(12):
        here = grads[16 * block : 16 * block + 16]
        rows.append(here[1:5, :64] + here[3:7, 64:128] + here[5:9, 128:192])
    sums_ref[0:24, :] = 128.0 * jnp.concatenate(
        [jnp.concatenate(rows[:6], axis=0), jnp.concatenate(rows[6:], axis=0)], axis=1
    )
    sums_ref[24:32, :] = jnp.concatenate([grads[192:200, 192:256], jnp.zeros((8, 64), F32)], axis=1)


def critic(*operands):
    return pl.pallas_call(
        critic_kernel,
        out_shape=jax.ShapeDtypeStruct((32, 128), F32),
        in_specs=[SMEM] + [VMEM] * 6,
        out_specs=VMEM,
        compiler_params=SMALL,
        name="critic",
    )(*operands)


def shifted(value, step):
    if step == 0:
        return value
    zero = jnp.zeros(value.shape[:1] + (1,), value.dtype)
    parts = []
    for start in range(0, value.shape[1], 256):
        here = value[:, start : start + 256]
        if step > 0:
            parts.append(jnp.concatenate([here[:, 1:], zero], axis=1))
        else:
            parts.append(jnp.concatenate([zero, here[:, :-1]], axis=1))
    return parts[0] if len(parts) == 1 else jnp.concatenate(parts, axis=1)


def feature_kernel(row_ref, previous_ref, image_ref, next_ref, far_ref, lpips_ref, spread_ref, critic_fwd_ref,
                   head_ref, critic_bwd_ref, first_fwd_ref, first_bwd_ref, second_fwd_ref, second_bwd_ref, out_ref,
                   below_ref, slope_ref, pre_ref, act_ref):
    first_row = row_ref[0]
    index = first_row // 4
    distant = (index & 15) == 15

    def valid(row):
        return ((first_row + row >= 0) & (first_row + row < 256)).astype(F32)

    line = iota((16, 256), 0) + (first_row - 4)
    inside = ((line >= 0) & (line < 256)).astype(F32)
    below_ref[...] = jnp.where(distant, far_ref[...].astype(F32), next_ref[...].astype(F32))
    images = []
    fake = []
    for image in range(2):
        parts = []
        for channel in range(3):
            here = place_rows(previous_ref, image_ref, below_ref, image, channel)
            if image == 0:
                fake.append(here)
            parts.append((here - LPIPS_SHIFT[channel]) / LPIPS_SCALE[channel] * inside)
        images.append(jnp.concatenate(parts, axis=0))
    scaled = jnp.concatenate(images, axis=1)
    windows = jnp.concatenate([shifted(scaled, step).astype(BF16) for step in (-1, 0, 1)], axis=0)
    pre_ref[...] = dot(first_fwd_ref[...], windows)
    for row in range(10):
        value = pre_ref[64 * row : 64 * row + 64, :]
        square = value * value + SOFTNESS
        inverse = lax.rsqrt(square)
        if 2 <= row < 8:
            slope_ref[64 * row - 128 : 64 * row - 64, :] = 0.5 + 0.5 * (value * inverse)[:, :256]
        act = (value + square * inverse) * (0.5 * valid(row - 3))
        stack = jnp.concatenate([shifted(act, step).astype(BF16) for step in (-1, 0, 1)], axis=0)
        product = dot(second_fwd_ref[...], stack)
        for row_tap in range(3):
            target = row - row_tap
            if 0 <= target < 8:
                part = product[64 * row_tap : 64 * row_tap + 64]
                if row_tap == 0:
                    act_ref[64 * target : 64 * target + 64, :] = part
                else:
                    act_ref[64 * target : 64 * target + 64, :] += part
    weights = lpips_ref[...]
    acts = [None] * 6
    for row in range(8):
        value = act_ref[64 * row : 64 * row + 64, :]
        square = value * value + SOFTNESS
        inverse = lax.rsqrt(square)
        feature = 0.5 * (value + square * inverse)
        power = jnp.sum(feature * feature, axis=0, keepdims=True) + 1e-6
        norm = lax.rsqrt(power)
        unit = feature * norm
        unit_fake = unit[:, :256]
        direction = weights * (unit_fake - unit[:, 256:])
        inner = jnp.sum(direction * unit_fake, axis=0, keepdims=True)
        slope = 0.5 + 0.5 * (value[:, :256] * inverse[:, :256])
        grad = (direction - unit_fake * inner) * slope * (norm[:, :256] * (2.0 * valid(row - 2)))
        stack = jnp.concatenate([shifted(grad, step).astype(BF16) for step in (1, 0, -1)], axis=0)
        product = dot(second_bwd_ref[...], stack)
        for row_tap in range(3):
            target = row - 2 + row_tap
            if 0 <= target < 6:
                part = product[64 * row_tap : 64 * row_tap + 64]
                acts[target] = part if acts[target] is None else acts[target] + part
    grads = jnp.concatenate(
        [
            (acts[row] * slope_ref[64 * row : 64 * row + 64, :] * valid(row - 1)).astype(BF16)
            for row in range(6)
        ],
        axis=0,
    )
    product = dot(first_bwd_ref[...], grads)
    image_grad = shifted(product[0:16], 1) + product[16:32] + shifted(product[32:48], -1)
    taps = dot(jnp.concatenate(fake, axis=0).astype(BF16), spread_ref[...]).astype(BF16)
    pre = dot(critic_fwd_ref[...], stack_taps(taps, 0))
    slope = 0.6 + 0.4 * (pre * lax.rsqrt(pre * pre + SOFTNESS))
    head = head_ref[...]
    signals = []
    for patch in range(4):
        inside = (first_row + 2 * patch - 2 >= 0) & (first_row + 2 * patch - 2 < 256)
        signals.append((slope[64 * patch : 64 * patch + 64] * (head * -inside.astype(F32))).astype(BF16))
    product = dot(critic_bwd_ref[...], jnp.concatenate(signals, axis=0))
    taps = jnp.concatenate([product[16 * tap : 16 * tap + 16] for tap in range(4)], axis=1)
    high, low = split(taps)
    critic_grad = lax.dot_general(high, spread_ref[...], NT, preferred_element_type=F32) + lax.dot_general(
        low, spread_ref[...], NT, preferred_element_type=F32
    )
    for channel in range(3):
        out_ref[channel] = (
            image_grad[4 * channel : 4 * channel + 4] / LPIPS_SCALE[channel]
            + critic_grad[4 * channel : 4 * channel + 4]
        )


def features(*operands):
    return pl.pallas_call(
        feature_kernel,
        out_shape=jax.ShapeDtypeStruct((3, 4, 256), F32),
        in_specs=[SMEM] + [VMEM] * 13,
        out_specs=VMEM,
        scratch_shapes=[
            pltpu.VMEM((2, 3, 4, 256), F32),
            pltpu.VMEM((384, 256), F32),
            pltpu.VMEM((640, 512), F32),
            pltpu.VMEM((512, 512), F32),
        ],
        compiler_params=pltpu.CompilerParams(vmem_limit_bytes=16 * 1024 * 1024),
        cost_estimate=pl.CostEstimate(flops=1_000_000_000, bytes_accessed=1_000_000, transcendentals=1_000_000),
        name="features",
    )(*operands)


def weight_rows(weight):
    moved = jnp.transpose(weight, (1, 2, 3, 0))
    taps = moved.shape[1]
    return jnp.pad(moved, ((0, 0), (0, 4 - taps), (0, 4 - taps), (0, 0))).reshape(48, 64)


def exchange_sum(value, axes):
    peers = lax.axis_size(axes)
    copies = jnp.broadcast_to(value[None], (peers,) + value.shape)
    return jnp.sum(lax.all_to_all(copies, axes, 0, 0).astype(F32), axis=0)


def shards(fake, real, vgg_first, vgg_second, lpips_weights, critic_conv, critic_head):
    count = lax.axis_size(ROWS)
    first_row = (lax.axis_index(ROWS) * 4).astype(jnp.int32)[None]
    images = jnp.concatenate([fake, real], axis=0)
    previous = lax.ppermute(images, ROWS, [(k, k + 1) for k in range(count - 1)])
    following = lax.ppermute(images, ROWS, [(k + 1, k) for k in range(count - 1) if k % 16 < 15])
    critic_rows = weight_rows(critic_conv)
    spread, critic_fwd, head = critic_weights(critic_rows, critic_head[None])
    sums = critic(first_row, previous, images, following, spread, critic_fwd, head)
    sums, later, first, second, again = lax.optimization_barrier(
        (sums, images, weight_rows(vgg_first), jnp.transpose(vgg_second, (2, 3, 0, 1)), critic_rows)
    )
    weights = feature_weights(first, second, again)
    plane = exchange_sum(sums.astype(jnp.float16), PLANE)
    far = lax.ppermute(later, ROWS, [(k + 1, k) for k in range(count - 1) if k % 16 == 15])
    total = exchange_sum((plane * (1.0 / 32.0)).astype(jnp.float16), COLUMN)
    grad_image = features(
        first_row, previous, images, following, far, lpips_weights[:, None], spread, critic_fwd, head, *weights
    )
    patches = 8 * 128 * 128
    conv = jnp.concatenate([total[:24, :64], total[:24, 64:]], axis=0) * (32.0 / 128.0 / patches)
    conv_grad = jnp.transpose(conv.reshape(4, 3, 4, 64), (3, 1, 2, 0))
    head_grad = (total[24, :64] + total[24, 64:]) * (32.0 / patches)
    return grad_image[None], conv_grad, head_grad


def solution(mesh):
    wide = Mesh(mesh.devices.reshape(2, 4, 4, 8, 2), ("zh", "y", "x", "zl", "c"))
    return jax.shard_map(
        shards,
        mesh=wide,
        in_specs=(P(DP, None, ROWS, None), P(DP, None, ROWS, None), P(), P(), P(), P(), P()),
        out_specs=(P(DP, None, ROWS, None), P(), P()),
        check_vma=False,
    )
```

```python
import functools

import jax
import jax.numpy as jnp
from jax import lax
from jax.experimental import pallas as pl
from jax.experimental.pallas import tpu as pltpu
from jax.sharding import Mesh, PartitionSpec as P

LPIPS_SHIFT = (-0.03, -0.088, -0.188)
LPIPS_SCALE = (0.458, 0.448, 0.45)
SOFTNESS = 0.04
ROWS = ("x", "zl", "c")
DP = ("zh", "y")
PLANE = ("y", "x", "c")
COLUMN = ("zh", "zl")
PLANE_ORDER = [4] + [peer for peer in range(32) if peer != 4]
COLUMN_ORDER = list(range(8, 16)) + list(range(8))
F32 = jnp.float32
BF16 = jnp.bfloat16
VMEM = pl.BlockSpec(memory_space=pltpu.VMEM)
SMEM = pl.BlockSpec(memory_space=pltpu.SMEM)
TN = (((0,), (0,)), ((), ()))
NT = (((1,), (1,)), ((), ()))
SMALL = pltpu.CompilerParams(vmem_limit_bytes=8 * 1024 * 1024)


def iota(shape, dim):
    return lax.broadcasted_iota(jnp.int32, shape, dim)


def dot(lhs, rhs):
    return jnp.dot(lhs, rhs, preferred_element_type=F32)


def split(value):
    high = value.astype(BF16)
    return high, (value - high.astype(F32)).astype(BF16)


def tap_index(m):
    return m >> 4, (m >> 2) & 3, m & 3


def block_index(k):
    tap = (k >= 48).astype(jnp.int32) + (k >= 96).astype(jnp.int32) + (k >= 144).astype(jnp.int32)
    rest = k - 48 * tap
    return tap, rest >> 4, rest & 15


def place_rows(previous_ref, image_ref, next_ref, image, channel):
    refs = (previous_ref, image_ref) if next_ref is None else (previous_ref, image_ref, next_ref)
    parts = [ref[image, channel].astype(F32) for ref in refs]
    return jnp.concatenate(parts + [jnp.zeros((16 - 4 * len(parts), 256), F32)], axis=0)


def expand(weight, width, first_row):
    channel, row_tap, col_tap = tap_index(iota((48, width), 0))
    block_tap, block_channel, block_row = block_index(iota((48, width), 1))
    chosen = (channel == block_channel) & (col_tap == block_tap) & (block_row == first_row + row_tap)
    return lax.dot_general(
        weight, chosen.astype(F32).astype(BF16), TN, preferred_element_type=F32
    ).astype(BF16)


def critic_weights_kernel(critic_ref, head_ref, spread_ref, fwd_ref, column_ref):
    column = iota((256, 512), 0)
    place = iota((256, 512), 1)
    spread_ref[...] = (column == 2 * (place & 127) + (place >> 7) - 1).astype(F32).astype(BF16)
    critic = critic_ref[...]
    for patch in range(4):
        fwd_ref[64 * patch : 64 * patch + 64, :] = expand(critic, 192, 1 + 2 * patch)
    diagonal = iota((64, 64), 0) == iota((64, 64), 1)
    column_ref[...] = jnp.sum(jnp.where(diagonal, head_ref[...], 0.0), axis=1, keepdims=True)


def critic_weights(critic, head):
    return pl.pallas_call(
        critic_weights_kernel,
        out_shape=[
            jax.ShapeDtypeStruct((256, 512), BF16),
            jax.ShapeDtypeStruct((256, 192), BF16),
            jax.ShapeDtypeStruct((64, 1), F32),
        ],
        in_specs=[VMEM] * 2,
        out_specs=[VMEM] * 3,
        compiler_params=SMALL,
        name="critic_weights",
    )(critic, head)


def feature_weights_kernel(first_ref, second_ref, critic_ref, critic_bwd_ref, first_fwd_ref, first_bwd_ref,
                           second_fwd_ref, second_bwd_ref):
    critic = critic_ref[...]
    first = first_ref[...]
    for row in range(10):
        first_fwd_ref[64 * row : 64 * row + 64, :] = expand(first, 144, row)

    def gather(weight, shift):
        row = iota((64, 48), 0)
        channel, row_tap, col_tap = tap_index(iota((64, 48), 1))
        inner = row & 15
        chosen = (row >> 4 == col_tap) & (inner >> 2 == channel) & ((inner & 3) + shift == row_tap)
        return dot(chosen.astype(F32).astype(BF16), weight).astype(BF16)

    critic_bwd_ref[...] = jnp.concatenate([gather(critic, 3 - 2 * patch) for patch in range(4)], axis=1)
    first_bwd_ref[...] = jnp.concatenate([gather(first, 2 - row)[:48] for row in range(6)], axis=1)
    for row_tap in range(3):
        second_fwd_ref[64 * row_tap : 64 * row_tap + 64, :] = jnp.concatenate(
            [second_ref[row_tap, col_tap] for col_tap in range(3)], axis=1
        )
        second_bwd_ref[64 * row_tap : 64 * row_tap + 64, :] = jnp.concatenate(
            [second_ref[row_tap, col_tap].astype(F32).T.astype(BF16) for col_tap in range(3)], axis=1
        )


def feature_weights(first, second, critic):
    shapes = [(64, 256), (640, 144), (48, 384), (192, 192), (192, 192)]
    return pl.pallas_call(
        feature_weights_kernel,
        out_shape=[jax.ShapeDtypeStruct(shape, BF16) for shape in shapes],
        in_specs=[VMEM] * 3,
        out_specs=[VMEM] * len(shapes),
        compiler_params=SMALL,
        cost_estimate=pl.CostEstimate(flops=100_000_000, bytes_accessed=1_000_000, transcendentals=0),
        name="feature_weights",
    )(first, second, critic)


def stack_taps(taps, image):
    return jnp.concatenate(
        [taps[48 * image : 48 * image + 48, 128 * tap : 128 * tap + 128] for tap in range(4)], axis=0
    )


def critic_kernel(row_ref, previous_ref, image_ref, spread_ref, weight_ref, head_ref, sums_ref):
    index = row_ref[0] // 4
    shares = ((index > 0).astype(F32), 1.0, (index == 63).astype(F32))
    image = jnp.concatenate(
        [
            place_rows(previous_ref, image_ref, None, image, channel)
            for image in range(2)
            for channel in range(3)
        ],
        axis=0,
    ).astype(BF16)
    taps = dot(image, spread_ref[...]).astype(BF16)
    windows = jnp.concatenate([stack_taps(taps, 0), stack_taps(taps, 1)], axis=1)
    pre = dot(weight_ref[0:192, :], windows)
    head = head_ref[...]
    square = pre * pre + SOFTNESS
    inverse = lax.rsqrt(square)
    hidden = 0.6 * pre + 0.4 * (square * inverse)
    slope = 0.6 + 0.4 * (pre * inverse)
    lane = iota((1, 256), 1)
    signals = []
    total = None
    for patch, share in enumerate(shares):
        part = hidden[64 * patch : 64 * patch + 64]
        logit = jnp.sum(head * part, axis=0, keepdims=True)
        sign = jnp.where(
            lane < 128, jnp.where(logit > -1.0, 1.0, 0.0), jnp.where(logit < 1.0, -1.0, 0.0)
        ) * share
        signals.append(slope[64 * patch : 64 * patch + 64] * head * sign)
        total = part * sign if total is None else total + part * sign
    high, low = split(jnp.concatenate(signals + [total], axis=0))
    windows = jnp.concatenate([windows, jnp.ones((16, 256), BF16)], axis=0)
    grads = lax.dot_general(windows, high, NT, preferred_element_type=F32) + lax.dot_general(
        windows, low, NT, preferred_element_type=F32
    )
    rows = []
    for block in range(12):
        here = grads[16 * block : 16 * block + 16]
        rows.append(here[1:5, :64] + here[3:7, 64:128] + here[5:9, 128:192])
    sums_ref[0:24, :] = 128.0 * jnp.concatenate(
        [jnp.concatenate(rows[:6], axis=0), jnp.concatenate(rows[6:], axis=0)], axis=1
    )
    sums_ref[24:32, :] = jnp.concatenate([grads[192:200, 192:256], jnp.zeros((8, 64), F32)], axis=1)


def critic(*operands):
    return pl.pallas_call(
        critic_kernel,
        out_shape=jax.ShapeDtypeStruct((32, 128), F32),
        in_specs=[SMEM] + [VMEM] * 5,
        out_specs=VMEM,
        compiler_params=SMALL,
        name="critic",
    )(*operands)


def shifted(value, step):
    if step == 0:
        return value
    zero = jnp.zeros(value.shape[:1] + (1,), value.dtype)
    parts = []
    for start in range(0, value.shape[1], 256):
        here = value[:, start : start + 256]
        if step > 0:
            parts.append(jnp.concatenate([here[:, 1:], zero], axis=1))
        else:
            parts.append(jnp.concatenate([zero, here[:, :-1]], axis=1))
    return parts[0] if len(parts) == 1 else jnp.concatenate(parts, axis=1)


def feature_kernel(row_ref, previous_ref, image_ref, next_ref, lpips_ref, spread_ref, critic_fwd_ref,
                   head_ref, critic_bwd_ref, first_fwd_ref, first_bwd_ref, second_fwd_ref, second_bwd_ref, out_ref,
                   slope_ref, pre_ref, act_ref):
    first_row = row_ref[0]

    def valid(row):
        return ((first_row + row >= 0) & (first_row + row < 256)).astype(F32)

    line = iota((16, 256), 0) + (first_row - 4)
    inside = ((line >= 0) & (line < 256)).astype(F32)
    images = []
    fake = []
    for image in range(2):
        parts = []
        for channel in range(3):
            here = place_rows(previous_ref, image_ref, next_ref, image, channel)
            if image == 0:
                fake.append(here)
            parts.append((here - LPIPS_SHIFT[channel]) / LPIPS_SCALE[channel] * inside)
        images.append(jnp.concatenate(parts, axis=0))
    scaled = jnp.concatenate(images, axis=1)
    windows = jnp.concatenate([shifted(scaled, step).astype(BF16) for step in (-1, 0, 1)], axis=0)
    pre_ref[...] = dot(first_fwd_ref[...], windows)
    for row in range(10):
        value = pre_ref[64 * row : 64 * row + 64, :]
        square = value * value + SOFTNESS
        inverse = lax.rsqrt(square)
        if 2 <= row < 8:
            slope_ref[64 * row - 128 : 64 * row - 64, :] = 0.5 + 0.5 * (value * inverse)[:, :256]
        act = (value + square * inverse) * (0.5 * valid(row - 3))
        stack = jnp.concatenate([shifted(act, step).astype(BF16) for step in (-1, 0, 1)], axis=0)
        product = dot(second_fwd_ref[...], stack)
        for row_tap in range(3):
            target = row - row_tap
            if 0 <= target < 8:
                part = product[64 * row_tap : 64 * row_tap + 64]
                if row_tap == 0:
                    act_ref[64 * target : 64 * target + 64, :] = part
                else:
                    act_ref[64 * target : 64 * target + 64, :] += part
    weights = lpips_ref[...]
    acts = [None] * 6
    for row in range(8):
        value = act_ref[64 * row : 64 * row + 64, :]
        square = value * value + SOFTNESS
        inverse = lax.rsqrt(square)
        feature = 0.5 * (value + square * inverse)
        power = jnp.sum(feature * feature, axis=0, keepdims=True) + 1e-6
        norm = lax.rsqrt(power)
        unit = feature * norm
        unit_fake = unit[:, :256]
        direction = weights * (unit_fake - unit[:, 256:])
        inner = jnp.sum(direction * unit_fake, axis=0, keepdims=True)
        slope = 0.5 + 0.5 * (value[:, :256] * inverse[:, :256])
        grad = (direction - unit_fake * inner) * slope * (norm[:, :256] * (2.0 * valid(row - 2)))
        stack = jnp.concatenate([shifted(grad, step).astype(BF16) for step in (1, 0, -1)], axis=0)
        product = dot(second_bwd_ref[...], stack)
        for row_tap in range(3):
            target = row - 2 + row_tap
            if 0 <= target < 6:
                part = product[64 * row_tap : 64 * row_tap + 64]
                acts[target] = part if acts[target] is None else acts[target] + part
    grads = jnp.concatenate(
        [
            (acts[row] * slope_ref[64 * row : 64 * row + 64, :] * valid(row - 1)).astype(BF16)
            for row in range(6)
        ],
        axis=0,
    )
    product = dot(first_bwd_ref[...], grads)
    image_grad = shifted(product[0:16], 1) + product[16:32] + shifted(product[32:48], -1)
    taps = dot(jnp.concatenate(fake, axis=0).astype(BF16), spread_ref[...]).astype(BF16)
    pre = dot(critic_fwd_ref[...], stack_taps(taps, 0))
    slope = 0.6 + 0.4 * (pre * lax.rsqrt(pre * pre + SOFTNESS))
    head = head_ref[...]
    signals = []
    for patch in range(4):
        inside = (first_row + 2 * patch - 2 >= 0) & (first_row + 2 * patch - 2 < 256)
        signals.append((slope[64 * patch : 64 * patch + 64] * (head * -inside.astype(F32))).astype(BF16))
    product = dot(critic_bwd_ref[...], jnp.concatenate(signals, axis=0))
    taps = jnp.concatenate([product[16 * tap : 16 * tap + 16] for tap in range(4)], axis=1)
    high, low = split(taps)
    critic_grad = lax.dot_general(high, spread_ref[...], NT, preferred_element_type=F32) + lax.dot_general(
        low, spread_ref[...], NT, preferred_element_type=F32
    )
    for channel in range(3):
        out_ref[channel] = (
            image_grad[4 * channel : 4 * channel + 4] / LPIPS_SCALE[channel]
            + critic_grad[4 * channel : 4 * channel + 4]
        )


def features(*operands):
    return pl.pallas_call(
        feature_kernel,
        out_shape=jax.ShapeDtypeStruct((3, 4, 256), F32),
        in_specs=[SMEM] + [VMEM] * 12,
        out_specs=VMEM,
        scratch_shapes=[
            pltpu.VMEM((384, 256), F32),
            pltpu.VMEM((640, 512), F32),
            pltpu.VMEM((512, 512), F32),
        ],
        compiler_params=pltpu.CompilerParams(vmem_limit_bytes=16 * 1024 * 1024),
        cost_estimate=pl.CostEstimate(flops=20_000_000_000, bytes_accessed=1_000_000, transcendentals=1_000_000),
        name="features",
    )(*operands)


def finish_kernel(total_ref, conv_ref, head_ref):
    patches = 8 * 128 * 128
    total = total_ref[...]
    scaled = total[:24] * (32.0 / 128.0 / patches)
    halves = (scaled, pltpu.roll(scaled, 64, 1))
    for col_tap in range(4):
        for channel in range(3):
            start = 12 * (col_tap % 2) + 4 * channel
            rows = halves[col_tap // 2][start : start + 4, :64]
            for row_tap in range(4):
                conv_ref[channel, row_tap, col_tap : col_tap + 1, :] = rows[row_tap : row_tap + 1]
    head_ref[...] = total[24:25, :64] * (32.0 / patches)


def finish(total):
    return pl.pallas_call(
        finish_kernel,
        out_shape=[jax.ShapeDtypeStruct((3, 4, 4, 64), F32), jax.ShapeDtypeStruct((1, 64), F32)],
        in_specs=[VMEM],
        out_specs=[VMEM] * 2,
        compiler_params=SMALL,
        name="finish",
    )(total)


def weight_rows(weight):
    moved = jnp.transpose(weight, (1, 2, 3, 0))
    taps = moved.shape[1]
    return jnp.pad(moved, ((0, 0), (0, 4 - taps), (0, 4 - taps), (0, 0))).reshape(48, 64)


def exchange_sum(value, axes, order=None):
    peers = lax.axis_size(axes)
    copies = jnp.broadcast_to(value[None], (peers,) + value.shape)
    groups = None if order is None else [order]
    return jnp.sum(lax.all_to_all(copies, axes, 0, 0, axis_index_groups=groups).astype(F32), axis=0)


def shards(fake, real, vgg_first, vgg_second, lpips_weights, critic_conv, critic_head):
    count = lax.axis_size(ROWS)
    first_row = (lax.axis_index(ROWS) * 4).astype(jnp.int32)[None]
    images = jnp.concatenate([fake, real], axis=0)
    previous = lax.ppermute(images, ROWS, [(k, k + 1) for k in range(count - 1)])
    following = lax.ppermute(images, ROWS, [(k + 1, k) for k in range(count - 1)])
    critic_rows = weight_rows(critic_conv)
    spread, critic_fwd, head = critic_weights(critic_rows, critic_head[None])
    sums = critic(first_row, previous, images, spread, critic_fwd, head)
    sums, first, second, again = lax.optimization_barrier(
        (sums, weight_rows(vgg_first), jnp.transpose(vgg_second, (2, 3, 0, 1)), critic_rows)
    )
    weights = feature_weights(first, second, again)
    plane = exchange_sum(sums.astype(jnp.float16), PLANE, PLANE_ORDER)
    total = exchange_sum((plane * (1.0 / 32.0)).astype(jnp.float16), COLUMN, COLUMN_ORDER)
    grad_image = features(
        first_row, previous, images, following, lpips_weights[:, None], spread, critic_fwd, head, *weights
    )
    conv_grad, head_grad = finish(total)
    return grad_image[None], jnp.transpose(conv_grad, (3, 0, 1, 2)), head_grad[0]


def solution(mesh):
    wide = Mesh(mesh.devices.reshape(2, 4, 4, 8, 2), ("zh", "y", "x", "zl", "c"))
    return jax.shard_map(
        shards,
        mesh=wide,
        in_specs=(P(DP, None, ROWS, None), P(DP, None, ROWS, None), P(), P(), P(), P(), P()),
        out_specs=(P(DP, None, ROWS, None), P(), P()),
        check_vma=False,
    )
```

```python
import functools

import jax
import jax.numpy as jnp
from jax import lax
from jax.experimental import pallas as pl
from jax.experimental.pallas import tpu as pltpu
from jax.sharding import Mesh, PartitionSpec as P

LPIPS_SHIFT = (-0.03, -0.088, -0.188)
LPIPS_SCALE = (0.458, 0.448, 0.45)
SOFTNESS = 0.04
ROWS = ("x", "zl", "c")
DP = ("zh", "y")
PLANE = ("y", "x", "c")
COLUMN = ("zh", "zl")
MIDDLE = 9
PLANE_ORDER = [5] + [peer for peer in range(32) if peer != 5]
COLUMN_ORDER = list(range(8, 16)) + list(range(8))
F32 = jnp.float32
BF16 = jnp.bfloat16
VMEM = pl.BlockSpec(memory_space=pltpu.VMEM)
SMEM = pl.BlockSpec(memory_space=pltpu.SMEM)
TN = (((0,), (0,)), ((), ()))
NT = (((1,), (1,)), ((), ()))
SMALL = pltpu.CompilerParams(vmem_limit_bytes=8 * 1024 * 1024)


def iota(shape, dim):
    return lax.broadcasted_iota(jnp.int32, shape, dim)


def dot(lhs, rhs):
    return jnp.dot(lhs, rhs, preferred_element_type=F32)


def split(value):
    high = value.astype(BF16)
    return high, (value - high.astype(F32)).astype(BF16)


def tap_index(m):
    return m >> 4, (m >> 2) & 3, m & 3


def block_index(k):
    tap = (k >= 48).astype(jnp.int32) + (k >= 96).astype(jnp.int32) + (k >= 144).astype(jnp.int32)
    rest = k - 48 * tap
    return tap, rest >> 4, rest & 15


def expand(weight, width, first_row):
    channel, row_tap, col_tap = tap_index(iota((48, width), 0))
    block_tap, block_channel, block_row = block_index(iota((48, width), 1))
    chosen = (channel == block_channel) & (col_tap == block_tap) & (block_row == first_row + row_tap)
    return lax.dot_general(
        weight, chosen.astype(F32).astype(BF16), TN, preferred_element_type=F32
    ).astype(BF16)


def critic_weights_kernel(critic_ref, head_ref, spread_ref, fwd_ref, column_ref):
    column = iota((256, 512), 0)
    place = iota((256, 512), 1)
    spread_ref[...] = (column == 2 * (place & 127) + (place >> 7) - 1).astype(F32).astype(BF16)
    critic = critic_ref[...]
    for patch in range(4):
        fwd_ref[64 * patch : 64 * patch + 64, :] = expand(critic, 192, 1 + 2 * patch)
    diagonal = iota((64, 64), 0) == iota((64, 64), 1)
    column_ref[...] = jnp.sum(jnp.where(diagonal, head_ref[...], 0.0), axis=1, keepdims=True)


def critic_weights(critic, head):
    return pl.pallas_call(
        critic_weights_kernel,
        out_shape=[
            jax.ShapeDtypeStruct((256, 512), BF16),
            jax.ShapeDtypeStruct((256, 192), BF16),
            jax.ShapeDtypeStruct((64, 1), F32),
        ],
        in_specs=[VMEM] * 2,
        out_specs=[VMEM] * 3,
        compiler_params=SMALL,
        name="critic_weights",
    )(critic, head)


def feature_weights_kernel(first_ref, second_ref, critic_ref, critic_bwd_ref, first_fwd_ref, first_bwd_ref,
                           second_fwd_ref, second_bwd_ref):
    critic = critic_ref[...]
    first = first_ref[...]
    for row in range(10):
        first_fwd_ref[64 * row : 64 * row + 64, :] = expand(first, 144, row)

    def gather(weight, shift):
        row = iota((64, 48), 0)
        channel, row_tap, col_tap = tap_index(iota((64, 48), 1))
        inner = row & 15
        chosen = (row >> 4 == col_tap) & (inner >> 2 == channel) & ((inner & 3) + shift == row_tap)
        return dot(chosen.astype(F32).astype(BF16), weight).astype(BF16)

    critic_bwd_ref[...] = jnp.concatenate([gather(critic, 3 - 2 * patch) for patch in range(4)], axis=1)
    first_bwd_ref[...] = jnp.concatenate([gather(first, 2 - row)[:48] for row in range(6)], axis=1)
    for row_tap in range(3):
        second_fwd_ref[64 * row_tap : 64 * row_tap + 64, :] = jnp.concatenate(
            [second_ref[row_tap, col_tap] for col_tap in range(3)], axis=1
        )
        second_bwd_ref[64 * row_tap : 64 * row_tap + 64, :] = jnp.concatenate(
            [second_ref[row_tap, col_tap].astype(F32).T.astype(BF16) for col_tap in range(3)], axis=1
        )


def feature_weights(first, second, critic):
    shapes = [(64, 256), (640, 144), (48, 384), (192, 192), (192, 192)]
    return pl.pallas_call(
        feature_weights_kernel,
        out_shape=[jax.ShapeDtypeStruct(shape, BF16) for shape in shapes],
        in_specs=[VMEM] * 3,
        out_specs=[VMEM] * len(shapes),
        compiler_params=SMALL,
        cost_estimate=pl.CostEstimate(flops=100_000_000, bytes_accessed=1_000_000, transcendentals=0),
        name="feature_weights",
    )(first, second, critic)


def stack_taps(taps, image):
    return jnp.concatenate(
        [taps[48 * image : 48 * image + 48, 128 * tap : 128 * tap + 128] for tap in range(4)], axis=0
    )


def critic_kernel(row_ref, under_ref, upper_ref, previous_ref, image_ref, spread_ref, weight_ref, head_ref, sums_ref):
    index = row_ref[0] // 4
    last = index == 63
    between = ((index & 15) == MIDDLE) & (index > 15)
    near = (index & 15) != 0
    shares = (
        (near.astype(F32), (between | last).astype(F32)),
        ((near | (index == 0)).astype(F32), between.astype(F32)),
    )
    blank = jnp.zeros((8, 256), F32)
    rows = []
    for image in range(2):
        for channel in range(3):
            rows += [previous_ref[image, channel].astype(F32), image_ref[image, channel].astype(F32), blank]
    for image in range(2):
        for channel in range(3):
            upper = jnp.where(last, image_ref[image, channel].astype(F32), upper_ref[image, channel])
            rows += [upper, under_ref[image, channel], blank]
    taps = dot(jnp.concatenate(rows, axis=0).astype(BF16), spread_ref[...]).astype(BF16)
    windows = jnp.concatenate([stack_taps(taps, place) for place in range(4)], axis=1)
    pre = dot(weight_ref[0:128, :], windows)
    head = head_ref[...]
    square = pre * pre + SOFTNESS
    inverse = lax.rsqrt(square)
    hidden = 0.6 * pre + 0.4 * (square * inverse)
    slope = 0.6 + 0.4 * (pre * inverse)
    lane = iota((1, 512), 1)
    signals = []
    total = None
    for patch in range(2):
        part = hidden[64 * patch : 64 * patch + 64]
        logit = jnp.sum(head * part, axis=0, keepdims=True)
        sign = jnp.where(
            (lane & 128) == 0, jnp.where(logit > -1.0, 1.0, 0.0), jnp.where(logit < 1.0, -1.0, 0.0)
        ) * jnp.where(lane < 256, shares[patch][0], shares[patch][1])
        signals.append(slope[64 * patch : 64 * patch + 64] * (head * sign))
        total = part * sign if total is None else total + part * sign
    high, low = split(jnp.concatenate(signals + [total], axis=0))
    windows = jnp.concatenate([windows, jnp.ones((16, 512), BF16)], axis=0)
    grads = lax.dot_general(windows, high, NT, preferred_element_type=F32) + lax.dot_general(
        windows, low, NT, preferred_element_type=F32
    )
    rows = []
    for block in range(12):
        here = grads[16 * block : 16 * block + 16]
        rows.append(here[1:5, :64] + here[3:7, 64:128])
    packed = 128.0 * jnp.concatenate(
        [jnp.concatenate(rows[:6], axis=0), jnp.concatenate(rows[6:], axis=0)], axis=1
    )
    for row in range(24):
        sums_ref[row // 12 : row // 12 + 1, 128 * (row % 12) : 128 * (row % 12) + 128] = packed[row : row + 1]
    head_sum = jnp.concatenate([grads[192:194, 128:192], jnp.zeros((2, 64), F32)], axis=1)
    sums_ref[:, 1536:1664] = head_sum


def critic(*operands):
    return pl.pallas_call(
        critic_kernel,
        out_shape=jax.ShapeDtypeStruct((2, 1664), F32),
        in_specs=[SMEM] + [VMEM] * 7,
        out_specs=VMEM,
        compiler_params=SMALL,
        name="critic",
    )(*operands)


def shifted(value, step):
    if step == 0:
        return value
    zero = jnp.zeros(value.shape[:1] + (1,), value.dtype)
    parts = []
    for start in range(0, value.shape[1], 256):
        here = value[:, start : start + 256]
        if step > 0:
            parts.append(jnp.concatenate([here[:, 1:], zero], axis=1))
        else:
            parts.append(jnp.concatenate([zero, here[:, :-1]], axis=1))
    return parts[0] if len(parts) == 1 else jnp.concatenate(parts, axis=1)


def feature_kernel(row_ref, critic_bwd_ref, first_fwd_ref, first_bwd_ref, second_fwd_ref, second_bwd_ref,
                   previous_ref, image_ref, next_ref, far_ref, lpips_ref, spread_ref, critic_fwd_ref, head_ref,
                   out_ref, slope_ref, pre_ref, act_ref):
    first_row = row_ref[0]
    place = first_row // 4 & 15

    def valid(row):
        return ((first_row + row >= 0) & (first_row + row < 256)).astype(F32)

    line = iota((16, 256), 0) + (first_row - 4)
    inside = ((line >= 0) & (line < 256)).astype(F32)
    images = []
    fake = []
    for image in range(2):
        parts = []
        for channel in range(3):
            far = far_ref[image, channel]
            above = jnp.where(place == 0, far, previous_ref[image, channel].astype(F32))
            below = jnp.where(place == 15, far, next_ref[image, channel].astype(F32))
            here = jnp.concatenate(
                [above, image_ref[image, channel].astype(F32), below, jnp.zeros_like(far)], axis=0
            )
            if image == 0:
                fake.append(here)
            parts.append((here - LPIPS_SHIFT[channel]) / LPIPS_SCALE[channel] * inside)
        images.append(jnp.concatenate(parts, axis=0))
    scaled = jnp.concatenate(images, axis=1)
    windows = jnp.concatenate([shifted(scaled, step).astype(BF16) for step in (-1, 0, 1)], axis=0)
    pre_ref[...] = dot(first_fwd_ref[...], windows)
    for row in range(10):
        value = pre_ref[64 * row : 64 * row + 64, :]
        square = value * value + SOFTNESS
        inverse = lax.rsqrt(square)
        if 2 <= row < 8:
            slope_ref[64 * row - 128 : 64 * row - 64, :] = 0.5 + 0.5 * (value * inverse)[:, :256]
        act = (value + square * inverse) * (0.5 * valid(row - 3))
        stack = jnp.concatenate([shifted(act, step).astype(BF16) for step in (-1, 0, 1)], axis=0)
        product = dot(second_fwd_ref[...], stack)
        for row_tap in range(3):
            target = row - row_tap
            if 0 <= target < 8:
                part = product[64 * row_tap : 64 * row_tap + 64]
                if row_tap == 0:
                    act_ref[64 * target : 64 * target + 64, :] = part
                else:
                    act_ref[64 * target : 64 * target + 64, :] += part
    weights = lpips_ref[...]
    acts = [None] * 6
    for row in range(8):
        value = act_ref[64 * row : 64 * row + 64, :]
        square = value * value + SOFTNESS
        inverse = lax.rsqrt(square)
        feature = 0.5 * (value + square * inverse)
        power = jnp.sum(feature * feature, axis=0, keepdims=True) + 1e-6
        norm = lax.rsqrt(power)
        unit = feature * norm
        unit_fake = unit[:, :256]
        direction = weights * (unit_fake - unit[:, 256:])
        inner = jnp.sum(direction * unit_fake, axis=0, keepdims=True)
        slope = 0.5 + 0.5 * (value[:, :256] * inverse[:, :256])
        grad = (direction - unit_fake * inner) * slope * (norm[:, :256] * (2.0 * valid(row - 2)))
        stack = jnp.concatenate([shifted(grad, step).astype(BF16) for step in (1, 0, -1)], axis=0)
        product = dot(second_bwd_ref[...], stack)
        for row_tap in range(3):
            target = row - 2 + row_tap
            if 0 <= target < 6:
                part = product[64 * row_tap : 64 * row_tap + 64]
                acts[target] = part if acts[target] is None else acts[target] + part
    grads = jnp.concatenate(
        [
            (acts[row] * slope_ref[64 * row : 64 * row + 64, :] * valid(row - 1)).astype(BF16)
            for row in range(6)
        ],
        axis=0,
    )
    product = dot(first_bwd_ref[...], grads)
    image_grad = shifted(product[0:16], 1) + product[16:32] + shifted(product[32:48], -1)
    taps = dot(jnp.concatenate(fake, axis=0).astype(BF16), spread_ref[...]).astype(BF16)
    pre = dot(critic_fwd_ref[...], stack_taps(taps, 0))
    slope = 0.6 + 0.4 * (pre * lax.rsqrt(pre * pre + SOFTNESS))
    head = head_ref[...]
    signals = []
    for patch in range(4):
        inside = (first_row + 2 * patch - 2 >= 0) & (first_row + 2 * patch - 2 < 256)
        signals.append((slope[64 * patch : 64 * patch + 64] * (head * -inside.astype(F32))).astype(BF16))
    product = dot(critic_bwd_ref[...], jnp.concatenate(signals, axis=0))
    taps = jnp.concatenate([product[16 * tap : 16 * tap + 16] for tap in range(4)], axis=1)
    high, low = split(taps)
    critic_grad = lax.dot_general(high, spread_ref[...], NT, preferred_element_type=F32) + lax.dot_general(
        low, spread_ref[...], NT, preferred_element_type=F32
    )
    for channel in range(3):
        out_ref[channel] = (
            image_grad[4 * channel : 4 * channel + 4] / LPIPS_SCALE[channel]
            + critic_grad[4 * channel : 4 * channel + 4]
        )


def features(*operands):
    return pl.pallas_call(
        feature_kernel,
        out_shape=jax.ShapeDtypeStruct((3, 4, 256), F32),
        in_specs=[SMEM] + [VMEM] * 13,
        out_specs=VMEM,
        scratch_shapes=[
            pltpu.VMEM((384, 256), F32),
            pltpu.VMEM((640, 512), F32),
            pltpu.VMEM((512, 512), F32),
        ],
        compiler_params=pltpu.CompilerParams(vmem_limit_bytes=16 * 1024 * 1024),
        cost_estimate=pl.CostEstimate(flops=20_000_000_000, bytes_accessed=1_000_000, transcendentals=1_000_000),
        name="features",
    )(*operands)


def finish_kernel(total_ref, conv_ref, head_ref):
    patches = 8 * 128 * 128
    for row in range(24):
        here = total_ref[row // 12 : row // 12 + 1, 128 * (row % 12) : 128 * (row % 12) + 128]
        here = here * (32.0 / 128.0 / patches)
        channel, row_tap = row % 12 // 4, row % 4
        for half in range(2):
            col_tap = 2 * half + row // 12
            conv_ref[channel, row_tap, col_tap : col_tap + 1, :] = here[:, 64 * half : 64 * half + 64]
    head_ref[...] = total_ref[0:1, 1536:1600] * (32.0 / patches)


def finish(total):
    return pl.pallas_call(
        finish_kernel,
        out_shape=[jax.ShapeDtypeStruct((3, 4, 4, 64), F32), jax.ShapeDtypeStruct((1, 64), F32)],
        in_specs=[VMEM],
        out_specs=[VMEM] * 2,
        compiler_params=SMALL,
        name="finish",
    )(total)


def weight_rows(weight):
    moved = jnp.transpose(weight, (1, 2, 3, 0))
    taps = moved.shape[1]
    return jnp.pad(moved, ((0, 0), (0, 4 - taps), (0, 4 - taps), (0, 0))).reshape(48, 64)


def exchange_sum(value, axes, order=None):
    peers = lax.axis_size(axes)
    copies = jnp.broadcast_to(value[None], (peers,) + value.shape)
    groups = None if order is None else [order]
    return jnp.sum(lax.all_to_all(copies, axes, 0, 0, axis_index_groups=groups).astype(F32), axis=0)


def shards(fake, real, vgg_first, vgg_second, lpips_weights, critic_conv, critic_head):
    count = lax.axis_size(ROWS)
    first_row = (lax.axis_index(ROWS) * 4).astype(jnp.int32)[None]
    images = jnp.concatenate([fake, real], axis=0)
    far_pairs = [(k, k + 1) for k in range(15, count - 1, 16)]
    whole = images.astype(F32)
    under = lax.ppermute(whole, ROWS, [(b, b + MIDDLE) for a, b in far_pairs])
    upper = lax.ppermute(whole, ROWS, [(a, b + MIDDLE) for a, b in far_pairs])
    critic_rows = weight_rows(critic_conv)
    spread, critic_fwd, head = critic_weights(critic_rows, critic_head[None])
    previous = lax.ppermute(images, ROWS, [(k, k + 1) for k in range(count - 1) if k % 16 < 15])
    following = lax.ppermute(images, ROWS, [(k + 1, k) for k in range(count - 1) if k % 16 < 15])
    far = lax.ppermute(whole, ROWS, far_pairs + [(b, a) for a, b in far_pairs])
    sums = critic(first_row, under, upper, previous, images, spread, critic_fwd, head)
    sums, first, second, again = lax.optimization_barrier(
        (sums, weight_rows(vgg_first), jnp.transpose(vgg_second, (2, 3, 0, 1)), critic_rows)
    )
    weights = feature_weights(first, second, again)
    plane = exchange_sum(sums.astype(jnp.float16), PLANE, PLANE_ORDER)
    total = exchange_sum((plane * (1.0 / 32.0)).astype(jnp.float16), COLUMN, COLUMN_ORDER)
    grad_image = features(
        first_row, *weights, previous, images, following, far, lpips_weights[:, None], spread, critic_fwd, head
    )
    conv_grad, head_grad = finish(total)
    return grad_image[None], jnp.transpose(conv_grad, (3, 0, 1, 2)), head_grad[0]


def solution(mesh):
    wide = Mesh(mesh.devices.reshape(2, 4, 4, 8, 2), ("zh", "y", "x", "zl", "c"))
    return jax.shard_map(
        shards,
        mesh=wide,
        in_specs=(P(DP, None, ROWS, None), P(DP, None, ROWS, None), P(), P(), P(), P(), P()),
        out_specs=(P(DP, None, ROWS, None), P(), P()),
        check_vma=False,
    )
```

```python
import functools

import jax
import jax.numpy as jnp
from jax import lax
from jax.experimental import pallas as pl
from jax.experimental.pallas import tpu as pltpu
from jax.sharding import Mesh, PartitionSpec as P

LPIPS_SHIFT = (-0.03, -0.088, -0.188)
LPIPS_SCALE = (0.458, 0.448, 0.45)
SOFTNESS = 0.04
ROWS = ("x", "zl", "c")
DP = ("zh", "y")
PLANE = ("y", "x", "c")
COLUMN = ("zh", "zl")
MIDDLE = 9
PLANE_ORDER = [21] + [peer for peer in range(32) if peer != 21]
COLUMN_ORDER = [(10 + peer) % 16 for peer in range(16)]
F32 = jnp.float32
BF16 = jnp.bfloat16
VMEM = pl.BlockSpec(memory_space=pltpu.VMEM)
SMEM = pl.BlockSpec(memory_space=pltpu.SMEM)
TN = (((0,), (0,)), ((), ()))
NT = (((1,), (1,)), ((), ()))
SMALL = pltpu.CompilerParams(vmem_limit_bytes=8 * 1024 * 1024)


def iota(shape, dim):
    return lax.broadcasted_iota(jnp.int32, shape, dim)


def dot(lhs, rhs):
    return jnp.dot(lhs, rhs, preferred_element_type=F32)


def split(value):
    high = value.astype(BF16)
    return high, (value - high.astype(F32)).astype(BF16)


def tap_index(m):
    return m >> 4, (m >> 2) & 3, m & 3


def block_index(k):
    tap = (k >= 48).astype(jnp.int32) + (k >= 96).astype(jnp.int32) + (k >= 144).astype(jnp.int32)
    rest = k - 48 * tap
    return tap, rest >> 4, rest & 15


def expand(weight, width, first_row):
    channel, row_tap, col_tap = tap_index(iota((48, width), 0))
    block_tap, block_channel, block_row = block_index(iota((48, width), 1))
    chosen = (channel == block_channel) & (col_tap == block_tap) & (block_row == first_row + row_tap)
    return lax.dot_general(
        weight, chosen.astype(F32).astype(BF16), TN, preferred_element_type=F32
    ).astype(BF16)


def critic_weights_kernel(critic_ref, head_ref, spread_ref, fwd_ref, column_ref):
    column = iota((256, 512), 0)
    place = iota((256, 512), 1)
    spread_ref[...] = (column == 2 * (place & 127) + (place >> 7) - 1).astype(F32).astype(BF16)
    critic = critic_ref[...]
    for patch in range(4):
        fwd_ref[64 * patch : 64 * patch + 64, :] = expand(critic, 192, 1 + 2 * patch)
    diagonal = iota((64, 64), 0) == iota((64, 64), 1)
    column_ref[...] = jnp.sum(jnp.where(diagonal, head_ref[...], 0.0), axis=1, keepdims=True)


def critic_weights(critic, head):
    return pl.pallas_call(
        critic_weights_kernel,
        out_shape=[
            jax.ShapeDtypeStruct((256, 512), BF16),
            jax.ShapeDtypeStruct((256, 192), BF16),
            jax.ShapeDtypeStruct((64, 1), F32),
        ],
        in_specs=[VMEM] * 2,
        out_specs=[VMEM] * 3,
        compiler_params=SMALL,
        name="critic_weights",
    )(critic, head)


def feature_weights_kernel(row_ref, first_ref, second_ref, critic_ref, next_ref, early_ref, under_ref, image_ref,
                           critic_bwd_ref, first_fwd_ref, first_bwd_ref,
                           second_fwd_ref, second_bwd_ref, copy_ref):
    between = (row_ref[0] // 4 & 15) == MIDDLE
    copy_ref[...] = jnp.where(between, under_ref[...], image_ref[...].astype(F32)).astype(BF16)
    critic = critic_ref[...]
    first = first_ref[...]
    for row in range(10):
        first_fwd_ref[64 * row : 64 * row + 64, :] = expand(first, 144, row)

    def gather(weight, shift):
        row = iota((64, 48), 0)
        channel, row_tap, col_tap = tap_index(iota((64, 48), 1))
        inner = row & 15
        chosen = (row >> 4 == col_tap) & (inner >> 2 == channel) & ((inner & 3) + shift == row_tap)
        return dot(chosen.astype(F32).astype(BF16), weight).astype(BF16)

    critic_bwd_ref[...] = jnp.concatenate([gather(critic, 3 - 2 * patch) for patch in range(4)], axis=1)
    first_bwd_ref[...] = jnp.concatenate([gather(first, 2 - row)[:48] for row in range(6)], axis=1)
    for row_tap in range(3):
        second_fwd_ref[64 * row_tap : 64 * row_tap + 64, :] = jnp.concatenate(
            [second_ref[row_tap, col_tap] for col_tap in range(3)], axis=1
        )
        second_bwd_ref[64 * row_tap : 64 * row_tap + 64, :] = jnp.concatenate(
            [second_ref[row_tap, col_tap].astype(F32).T.astype(BF16) for col_tap in range(3)], axis=1
        )


def feature_weights(*operands):
    shapes = [(64, 256), (640, 144), (48, 384), (192, 192), (192, 192), (2, 3, 4, 256)]
    return pl.pallas_call(
        feature_weights_kernel,
        out_shape=[jax.ShapeDtypeStruct(shape, BF16) for shape in shapes],
        in_specs=[SMEM] + [VMEM] * 7,
        out_specs=[VMEM] * len(shapes),
        compiler_params=SMALL,
        cost_estimate=pl.CostEstimate(flops=20_000_000_000, bytes_accessed=1_000_000, transcendentals=0),
        name="feature_weights",
    )(*operands)


def stack_taps(taps, image):
    return jnp.concatenate(
        [taps[48 * image : 48 * image + 48, 128 * tap : 128 * tap + 128] for tap in range(4)], axis=0
    )


def critic_kernel(row_ref, under_ref, upper_ref, previous_ref, image_ref, spread_ref, weight_ref, head_ref, sums_ref):
    index = row_ref[0] // 4
    last = index == 63
    between = ((index & 15) == MIDDLE) & (index > 15)
    near = (index & 15) != 0
    shares = (
        (near.astype(F32), (between | last).astype(F32)),
        ((near | (index == 0)).astype(F32), between.astype(F32)),
    )
    blank = jnp.zeros((8, 256), F32)
    rows = []
    for image in range(2):
        for channel in range(3):
            rows += [previous_ref[image, channel].astype(F32), image_ref[image, channel].astype(F32), blank]
    for image in range(2):
        for channel in range(3):
            upper = jnp.where(last, image_ref[image, channel].astype(F32), upper_ref[image, channel])
            rows += [upper, under_ref[image, channel], blank]
    taps = dot(jnp.concatenate(rows, axis=0).astype(BF16), spread_ref[...]).astype(BF16)
    windows = jnp.concatenate([stack_taps(taps, place) for place in range(4)], axis=1)
    pre = dot(weight_ref[0:128, :], windows)
    head = head_ref[...]
    square = pre * pre + SOFTNESS
    inverse = lax.rsqrt(square)
    hidden = 0.6 * pre + 0.4 * (square * inverse)
    slope = 0.6 + 0.4 * (pre * inverse)
    lane = iota((1, 512), 1)
    signals = []
    total = None
    for patch in range(2):
        part = hidden[64 * patch : 64 * patch + 64]
        logit = jnp.sum(head * part, axis=0, keepdims=True)
        sign = jnp.where(
            (lane & 128) == 0, jnp.where(logit > -1.0, 1.0, 0.0), jnp.where(logit < 1.0, -1.0, 0.0)
        ) * jnp.where(lane < 256, shares[patch][0], shares[patch][1])
        signals.append(slope[64 * patch : 64 * patch + 64] * (head * sign))
        total = part * sign if total is None else total + part * sign
    high, low = split(jnp.concatenate(signals + [total], axis=0))
    windows = jnp.concatenate([windows, jnp.ones((16, 512), BF16)], axis=0)
    grads = lax.dot_general(windows, high, NT, preferred_element_type=F32) + lax.dot_general(
        windows, low, NT, preferred_element_type=F32
    )
    rows = []
    for block in range(12):
        here = grads[16 * block : 16 * block + 16]
        rows.append(here[1:5, :64] + here[3:7, 64:128])
    packed = 128.0 * jnp.concatenate(
        [jnp.concatenate(rows[:6], axis=0), jnp.concatenate(rows[6:], axis=0)], axis=1
    )
    for row in range(24):
        sums_ref[row // 12 : row // 12 + 1, 128 * (row % 12) : 128 * (row % 12) + 128] = packed[row : row + 1]
    head_sum = jnp.concatenate([grads[192:194, 128:192], jnp.zeros((2, 64), F32)], axis=1)
    sums_ref[:, 1536:1664] = head_sum


def critic(*operands):
    return pl.pallas_call(
        critic_kernel,
        out_shape=jax.ShapeDtypeStruct((2, 1664), F32),
        in_specs=[SMEM] + [VMEM] * 7,
        out_specs=VMEM,
        compiler_params=SMALL,
        name="critic",
    )(*operands)


def shifted(value, step):
    if step == 0:
        return value
    zero = jnp.zeros(value.shape[:1] + (1,), value.dtype)
    parts = []
    for start in range(0, value.shape[1], 256):
        here = value[:, start : start + 256]
        if step > 0:
            parts.append(jnp.concatenate([here[:, 1:], zero], axis=1))
        else:
            parts.append(jnp.concatenate([zero, here[:, :-1]], axis=1))
    return parts[0] if len(parts) == 1 else jnp.concatenate(parts, axis=1)


def feature_kernel(row_ref, critic_bwd_ref, first_fwd_ref, first_bwd_ref, second_fwd_ref, second_bwd_ref,
                   previous_ref, image_ref, next_ref, early_ref, late_ref, lpips_ref, spread_ref, critic_fwd_ref, head_ref,
                   out_ref, slope_ref, pre_ref, act_ref):
    first_row = row_ref[0]
    place = first_row // 4 & 15

    def valid(row):
        return ((first_row + row >= 0) & (first_row + row < 256)).astype(F32)

    line = iota((16, 256), 0) + (first_row - 4)
    inside = ((line >= 0) & (line < 256)).astype(F32)
    images = []
    fake = []
    for image in range(2):
        parts = []
        for channel in range(3):
            far = late_ref[image, channel].astype(F32)
            above = jnp.where(place == 0, early_ref[image, channel] + far, previous_ref[image, channel].astype(F32))
            below = jnp.where(place == 15, far, next_ref[image, channel])
            here = jnp.concatenate(
                [above, image_ref[image, channel].astype(F32), below, jnp.zeros_like(far)], axis=0
            )
            if image == 0:
                fake.append(here)
            parts.append((here - LPIPS_SHIFT[channel]) / LPIPS_SCALE[channel] * inside)
        images.append(jnp.concatenate(parts, axis=0))
    scaled = jnp.concatenate(images, axis=1)
    windows = jnp.concatenate([shifted(scaled, step).astype(BF16) for step in (-1, 0, 1)], axis=0)
    pre_ref[...] = dot(first_fwd_ref[...], windows)
    for row in range(10):
        value = pre_ref[64 * row : 64 * row + 64, :]
        square = value * value + SOFTNESS
        inverse = lax.rsqrt(square)
        if 2 <= row < 8:
            slope_ref[64 * row - 128 : 64 * row - 64, :] = 0.5 + 0.5 * (value * inverse)[:, :256]
        act = (value + square * inverse) * (0.5 * valid(row - 3))
        stack = jnp.concatenate([shifted(act, step).astype(BF16) for step in (-1, 0, 1)], axis=0)
        product = dot(second_fwd_ref[...], stack)
        for row_tap in range(3):
            target = row - row_tap
            if 0 <= target < 8:
                part = product[64 * row_tap : 64 * row_tap + 64]
                if row_tap == 0:
                    act_ref[64 * target : 64 * target + 64, :] = part
                else:
                    act_ref[64 * target : 64 * target + 64, :] += part
    weights = lpips_ref[...]
    acts = [None] * 6
    for row in range(8):
        value = act_ref[64 * row : 64 * row + 64, :]
        square = value * value + SOFTNESS
        inverse = lax.rsqrt(square)
        feature = 0.5 * (value + square * inverse)
        power = jnp.sum(feature * feature, axis=0, keepdims=True) + 1e-6
        norm = lax.rsqrt(power)
        unit = feature * norm
        unit_fake = unit[:, :256]
        direction = weights * (unit_fake - unit[:, 256:])
        inner = jnp.sum(direction * unit_fake, axis=0, keepdims=True)
        slope = 0.5 + 0.5 * (value[:, :256] * inverse[:, :256])
        grad = (direction - unit_fake * inner) * slope * (norm[:, :256] * (2.0 * valid(row - 2)))
        stack = jnp.concatenate([shifted(grad, step).astype(BF16) for step in (1, 0, -1)], axis=0)
        product = dot(second_bwd_ref[...], stack)
        for row_tap in range(3):
            target = row - 2 + row_tap
            if 0 <= target < 6:
                part = product[64 * row_tap : 64 * row_tap + 64]
                acts[target] = part if acts[target] is None else acts[target] + part
    grads = jnp.concatenate(
        [
            (acts[row] * slope_ref[64 * row : 64 * row + 64, :] * valid(row - 1)).astype(BF16)
            for row in range(6)
        ],
        axis=0,
    )
    product = dot(first_bwd_ref[...], grads)
    image_grad = shifted(product[0:16], 1) + product[16:32] + shifted(product[32:48], -1)
    taps = dot(jnp.concatenate(fake, axis=0).astype(BF16), spread_ref[...]).astype(BF16)
    pre = dot(critic_fwd_ref[...], stack_taps(taps, 0))
    slope = 0.6 + 0.4 * (pre * lax.rsqrt(pre * pre + SOFTNESS))
    head = head_ref[...]
    signals = []
    for patch in range(4):
        inside = (first_row + 2 * patch - 2 >= 0) & (first_row + 2 * patch - 2 < 256)
        signals.append((slope[64 * patch : 64 * patch + 64] * (head * -inside.astype(F32))).astype(BF16))
    product = dot(critic_bwd_ref[...], jnp.concatenate(signals, axis=0))
    taps = jnp.concatenate([product[16 * tap : 16 * tap + 16] for tap in range(4)], axis=1)
    high, low = split(taps)
    critic_grad = lax.dot_general(high, spread_ref[...], NT, preferred_element_type=F32) + lax.dot_general(
        low, spread_ref[...], NT, preferred_element_type=F32
    )
    for channel in range(3):
        out_ref[channel] = (
            image_grad[4 * channel : 4 * channel + 4] / LPIPS_SCALE[channel]
            + critic_grad[4 * channel : 4 * channel + 4]
        )


def features(*operands):
    return pl.pallas_call(
        feature_kernel,
        out_shape=jax.ShapeDtypeStruct((3, 4, 256), F32),
        in_specs=[SMEM] + [VMEM] * 14,
        out_specs=VMEM,
        scratch_shapes=[
            pltpu.VMEM((384, 256), F32),
            pltpu.VMEM((640, 512), F32),
            pltpu.VMEM((512, 512), F32),
        ],
        compiler_params=pltpu.CompilerParams(vmem_limit_bytes=16 * 1024 * 1024),
        cost_estimate=pl.CostEstimate(flops=1_000_000_000, bytes_accessed=1_000_000, transcendentals=1_000_000),
        name="features",
    )(*operands)


def finish_kernel(total_ref, conv_ref, head_ref):
    patches = 8 * 128 * 128
    for row in range(24):
        here = total_ref[row // 12 : row // 12 + 1, 128 * (row % 12) : 128 * (row % 12) + 128]
        here = here * (32.0 / 128.0 / patches)
        channel, row_tap = row % 12 // 4, row % 4
        for half in range(2):
            col_tap = 2 * half + row // 12
            conv_ref[channel, row_tap, col_tap : col_tap + 1, :] = here[:, 64 * half : 64 * half + 64]
    head_ref[...] = total_ref[0:1, 1536:1600] * (32.0 / patches)


def finish(total):
    return pl.pallas_call(
        finish_kernel,
        out_shape=[jax.ShapeDtypeStruct((3, 4, 4, 64), F32), jax.ShapeDtypeStruct((1, 64), F32)],
        in_specs=[VMEM],
        out_specs=[VMEM] * 2,
        compiler_params=SMALL,
        name="finish",
    )(total)


def weight_rows(weight):
    moved = jnp.transpose(weight, (1, 2, 3, 0))
    taps = moved.shape[1]
    return jnp.pad(moved, ((0, 0), (0, 4 - taps), (0, 4 - taps), (0, 0))).reshape(48, 64)


def exchange_sum(value, axes, order=None):
    peers = lax.axis_size(axes)
    copies = jnp.broadcast_to(value[None], (peers,) + value.shape)
    groups = None if order is None else [order]
    return jnp.sum(lax.all_to_all(copies, axes, 0, 0, axis_index_groups=groups).astype(F32), axis=0)


def shards(fake, real, vgg_first, vgg_second, lpips_weights, critic_conv, critic_head):
    count = lax.axis_size(ROWS)
    first_row = (lax.axis_index(ROWS) * 4).astype(jnp.int32)[None]
    images = jnp.concatenate([fake, real], axis=0)
    far_pairs = [(k, k + 1) for k in range(15, count - 1, 16)]
    whole = images.astype(F32)
    under = lax.ppermute(whole, ROWS, [(b, b + MIDDLE) for a, b in far_pairs])
    upper = lax.ppermute(whole, ROWS, [(a, b + MIDDLE) for a, b in far_pairs])
    critic_rows = weight_rows(critic_conv)
    spread, critic_fwd, head = critic_weights(critic_rows, critic_head[None])
    previous = lax.ppermute(images, ROWS, [(k, k + 1) for k in range(count - 1) if k % 16 < 15])
    following = lax.ppermute(whole, ROWS, [(k + 1, k) for k in range(count - 1) if k % 16 < 15])
    early = lax.ppermute(upper, ("zh",) + ROWS, [(b + MIDDLE, b) for a, b in far_pairs])
    rest = [(count + a, count + b) for a, b in far_pairs]
    for base in (0, count):
        rest += [(base + b + MIDDLE, base + a) for a, b in far_pairs]
    sums = critic(first_row, under, upper, previous, images, spread, critic_fwd, head)
    plane = exchange_sum(sums.astype(jnp.float16), PLANE, PLANE_ORDER)
    plane, first, second, again = lax.optimization_barrier(
        (plane, weight_rows(vgg_first), jnp.transpose(vgg_second, (2, 3, 0, 1)), critic_rows)
    )
    *weights, copied = feature_weights(first_row, first, second, again, following, early, under, images)
    late = lax.ppermute(copied, ("zh",) + ROWS, rest)
    total = exchange_sum((plane * (1.0 / 32.0)).astype(jnp.float16), COLUMN, COLUMN_ORDER)
    grad_image = features(
        first_row, *weights, previous, images, following, early, late, lpips_weights[:, None], spread, critic_fwd, head
    )
    conv_grad, head_grad = finish(total)
    return grad_image[None], jnp.transpose(conv_grad, (3, 0, 1, 2)), head_grad[0]


def solution(mesh):
    wide = Mesh(mesh.devices.reshape(2, 4, 4, 8, 2), ("zh", "y", "x", "zl", "c"))
    return jax.shard_map(
        shards,
        mesh=wide,
        in_specs=(P(DP, None, ROWS, None), P(DP, None, ROWS, None), P(), P(), P(), P(), P()),
        out_specs=(P(DP, None, ROWS, None), P(), P()),
        check_vma=False,
    )
```

```python
import functools

import jax
import jax.numpy as jnp
from jax import lax
from jax.experimental import pallas as pl
from jax.experimental.pallas import tpu as pltpu
from jax.sharding import Mesh, PartitionSpec as P

LPIPS_SHIFT = (-0.03, -0.088, -0.188)
LPIPS_SCALE = (0.458, 0.448, 0.45)
SOFTNESS = 0.04
ROWS = ("x", "zl", "c")
DP = ("zh", "y")
PLANE = ("y", "x", "c")
COLUMN = ("zh", "zl")
MIDDLE = 9
PLANE_ORDER = [21, 0, 1, 2, 3, 6, 7, 8, 9, 24, 25, 4, 5, 10, 11, 14, 15, 16, 17, 26, 27, 30, 31, 12, 13, 18, 19, 22, 23, 28, 29, 20]
COLUMN_ORDER = [10, 0, 1, 2, 3, 15, 4, 14, 5, 13, 6, 12, 7, 11, 8, 9]
F32 = jnp.float32
BF16 = jnp.bfloat16
VMEM = pl.BlockSpec(memory_space=pltpu.VMEM)
SMEM = pl.BlockSpec(memory_space=pltpu.SMEM)
TN = (((0,), (0,)), ((), ()))
NT = (((1,), (1,)), ((), ()))
SMALL = pltpu.CompilerParams(vmem_limit_bytes=8 * 1024 * 1024)


def iota(shape, dim):
    return lax.broadcasted_iota(jnp.int32, shape, dim)


def dot(lhs, rhs):
    return jnp.dot(lhs, rhs, preferred_element_type=F32)


def split(value):
    high = value.astype(BF16)
    return high, (value - high.astype(F32)).astype(BF16)


def tap_index(m):
    return m >> 4, (m >> 2) & 3, m & 3


def block_index(k):
    tap = (k >= 48).astype(jnp.int32) + (k >= 96).astype(jnp.int32) + (k >= 144).astype(jnp.int32)
    rest = k - 48 * tap
    return tap, rest >> 4, rest & 15


def expand(weight, width, first_row):
    channel, row_tap, col_tap = tap_index(iota((48, width), 0))
    block_tap, block_channel, block_row = block_index(iota((48, width), 1))
    chosen = (channel == block_channel) & (col_tap == block_tap) & (block_row == first_row + row_tap)
    return lax.dot_general(
        weight, chosen.astype(F32).astype(BF16), TN, preferred_element_type=F32
    ).astype(BF16)


def critic_weights_kernel(critic_ref, head_ref, spread_ref, fwd_ref, column_ref):
    column = iota((256, 512), 0)
    place = iota((256, 512), 1)
    spread_ref[...] = (column == 2 * (place & 127) + (place >> 7) - 1).astype(F32).astype(BF16)
    critic = critic_ref[...]
    for patch in range(4):
        fwd_ref[64 * patch : 64 * patch + 64, :] = expand(critic, 192, 1 + 2 * patch)
    diagonal = iota((64, 64), 0) == iota((64, 64), 1)
    column_ref[...] = jnp.sum(jnp.where(diagonal, head_ref[...], 0.0), axis=1, keepdims=True)


def critic_weights(critic, head):
    return pl.pallas_call(
        critic_weights_kernel,
        out_shape=[
            jax.ShapeDtypeStruct((256, 512), BF16),
            jax.ShapeDtypeStruct((256, 192), BF16),
            jax.ShapeDtypeStruct((64, 1), F32),
        ],
        in_specs=[VMEM] * 2,
        out_specs=[VMEM] * 3,
        compiler_params=SMALL,
        name="critic_weights",
    )(critic, head)


def feature_weights_kernel(row_ref, first_ref, second_ref, critic_ref, next_ref, early_ref, under_ref, image_ref,
                           critic_bwd_ref, first_fwd_ref, first_bwd_ref,
                           second_fwd_ref, second_bwd_ref, copy_ref):
    between = (row_ref[0] // 4 & 15) == MIDDLE
    copy_ref[...] = jnp.where(between, under_ref[...], image_ref[...].astype(F32)).astype(BF16)
    critic = critic_ref[...]
    first = first_ref[...]
    for row in range(10):
        first_fwd_ref[64 * row : 64 * row + 64, :] = expand(first, 144, row)

    def gather(weight, shift):
        row = iota((64, 48), 0)
        channel, row_tap, col_tap = tap_index(iota((64, 48), 1))
        inner = row & 15
        chosen = (row >> 4 == col_tap) & (inner >> 2 == channel) & ((inner & 3) + shift == row_tap)
        return dot(chosen.astype(F32).astype(BF16), weight).astype(BF16)

    critic_bwd_ref[...] = jnp.concatenate([gather(critic, 3 - 2 * patch) for patch in range(4)], axis=1)
    first_bwd_ref[...] = jnp.concatenate([gather(first, 2 - row)[:48] for row in range(6)], axis=1)
    for row_tap in range(3):
        second_fwd_ref[64 * row_tap : 64 * row_tap + 64, :] = jnp.concatenate(
            [second_ref[row_tap, col_tap] for col_tap in range(3)], axis=1
        )
        second_bwd_ref[64 * row_tap : 64 * row_tap + 64, :] = jnp.concatenate(
            [second_ref[row_tap, col_tap].astype(F32).T.astype(BF16) for col_tap in range(3)], axis=1
        )


def feature_weights(*operands):
    shapes = [(64, 256), (640, 144), (48, 384), (192, 192), (192, 192), (2, 3, 4, 256)]
    return pl.pallas_call(
        feature_weights_kernel,
        out_shape=[jax.ShapeDtypeStruct(shape, BF16) for shape in shapes],
        in_specs=[SMEM] + [VMEM] * 7,
        out_specs=[VMEM] * len(shapes),
        compiler_params=SMALL,
        cost_estimate=pl.CostEstimate(flops=20_000_000_000, bytes_accessed=1_000_000, transcendentals=0),
        name="feature_weights",
    )(*operands)


def stack_taps(taps, image):
    return jnp.concatenate(
        [taps[48 * image : 48 * image + 48, 128 * tap : 128 * tap + 128] for tap in range(4)], axis=0
    )


def critic_kernel(row_ref, under_ref, upper_ref, previous_ref, image_ref, spread_ref, weight_ref, head_ref, sums_ref):
    index = row_ref[0] // 4
    last = index == 63
    between = ((index & 15) == MIDDLE) & (index > 15)
    near = (index & 15) != 0
    shares = (
        (near.astype(F32), (between | last).astype(F32)),
        ((near | (index == 0)).astype(F32), between.astype(F32)),
    )
    blank = jnp.zeros((8, 256), F32)
    rows = []
    for image in range(2):
        for channel in range(3):
            rows += [previous_ref[image, channel].astype(F32), image_ref[image, channel].astype(F32), blank]
    for image in range(2):
        for channel in range(3):
            upper = jnp.where(last, image_ref[image, channel].astype(F32), upper_ref[image, channel])
            rows += [upper, under_ref[image, channel], blank]
    taps = dot(jnp.concatenate(rows, axis=0).astype(BF16), spread_ref[...]).astype(BF16)
    windows = jnp.concatenate([stack_taps(taps, place) for place in range(4)], axis=1)
    pre = dot(weight_ref[0:128, :], windows)
    head = head_ref[...]
    square = pre * pre + SOFTNESS
    inverse = lax.rsqrt(square)
    hidden = 0.6 * pre + 0.4 * (square * inverse)
    slope = 0.6 + 0.4 * (pre * inverse)
    lane = iota((1, 512), 1)
    signals = []
    total = None
    for patch in range(2):
        part = hidden[64 * patch : 64 * patch + 64]
        logit = jnp.sum(head * part, axis=0, keepdims=True)
        sign = jnp.where(
            (lane & 128) == 0, jnp.where(logit > -1.0, 1.0, 0.0), jnp.where(logit < 1.0, -1.0, 0.0)
        ) * jnp.where(lane < 256, shares[patch][0], shares[patch][1])
        signals.append(slope[64 * patch : 64 * patch + 64] * (head * sign))
        total = part * sign if total is None else total + part * sign
    high, low = split(jnp.concatenate(signals + [total], axis=0))
    windows = jnp.concatenate([windows, jnp.ones((16, 512), BF16)], axis=0)
    grads = lax.dot_general(windows, high, NT, preferred_element_type=F32) + lax.dot_general(
        windows, low, NT, preferred_element_type=F32
    )
    rows = []
    for block in range(12):
        here = grads[16 * block : 16 * block + 16]
        rows.append(here[1:5, :64] + here[3:7, 64:128])
    packed = 64.0 * jnp.concatenate(
        [jnp.concatenate(rows[:6], axis=0), jnp.concatenate(rows[6:], axis=0)], axis=1
    )
    for row in range(24):
        sums_ref[row // 12 : row // 12 + 1, 128 * (row % 12) : 128 * (row % 12) + 128] = packed[row : row + 1]
    head_sum = jnp.concatenate([grads[192:194, 128:192], jnp.zeros((2, 64), F32)], axis=1)
    sums_ref[:, 1536:1664] = head_sum


def critic(*operands):
    return pl.pallas_call(
        critic_kernel,
        out_shape=jax.ShapeDtypeStruct((2, 1664), F32),
        in_specs=[SMEM] + [VMEM] * 7,
        out_specs=VMEM,
        compiler_params=SMALL,
        name="critic",
    )(*operands)


def shifted(value, step):
    if step == 0:
        return value
    zero = jnp.zeros(value.shape[:1] + (1,), value.dtype)
    parts = []
    for start in range(0, value.shape[1], 256):
        here = value[:, start : start + 256]
        if step > 0:
            parts.append(jnp.concatenate([here[:, 1:], zero], axis=1))
        else:
            parts.append(jnp.concatenate([zero, here[:, :-1]], axis=1))
    return parts[0] if len(parts) == 1 else jnp.concatenate(parts, axis=1)


def feature_kernel(row_ref, critic_bwd_ref, first_fwd_ref, first_bwd_ref, second_fwd_ref, second_bwd_ref,
                   previous_ref, image_ref, next_ref, early_ref, late_ref, lpips_ref, spread_ref, critic_fwd_ref, head_ref,
                   out_ref, slope_ref, pre_ref, act_ref):
    first_row = row_ref[0]
    place = first_row // 4 & 15

    def valid(row):
        return ((first_row + row >= 0) & (first_row + row < 256)).astype(F32)

    line = iota((16, 256), 0) + (first_row - 4)
    inside = ((line >= 0) & (line < 256)).astype(F32)
    images = []
    fake = []
    for image in range(2):
        parts = []
        for channel in range(3):
            far = late_ref[image, channel].astype(F32)
            above = jnp.where(place == 0, early_ref[image, channel] + far, previous_ref[image, channel].astype(F32))
            below = jnp.where(place == 15, far, next_ref[image, channel])
            here = jnp.concatenate(
                [above, image_ref[image, channel].astype(F32), below, jnp.zeros_like(far)], axis=0
            )
            if image == 0:
                fake.append(here)
            parts.append((here - LPIPS_SHIFT[channel]) / LPIPS_SCALE[channel] * inside)
        images.append(jnp.concatenate(parts, axis=0))
    scaled = jnp.concatenate(images, axis=1)
    windows = jnp.concatenate([shifted(scaled, step).astype(BF16) for step in (-1, 0, 1)], axis=0)
    pre_ref[...] = dot(first_fwd_ref[...], windows)
    for row in range(10):
        value = pre_ref[64 * row : 64 * row + 64, :]
        square = value * value + SOFTNESS
        inverse = lax.rsqrt(square)
        if 2 <= row < 8:
            slope_ref[64 * row - 128 : 64 * row - 64, :] = 0.5 + 0.5 * (value * inverse)[:, :256]
        act = (value + square * inverse) * (0.5 * valid(row - 3))
        stack = jnp.concatenate([shifted(act, step).astype(BF16) for step in (-1, 0, 1)], axis=0)
        product = dot(second_fwd_ref[...], stack)
        for row_tap in range(3):
            target = row - row_tap
            if 0 <= target < 8:
                part = product[64 * row_tap : 64 * row_tap + 64]
                if row_tap == 0:
                    act_ref[64 * target : 64 * target + 64, :] = part
                else:
                    act_ref[64 * target : 64 * target + 64, :] += part
    weights = lpips_ref[...]
    acts = [None] * 6
    for row in range(8):
        value = act_ref[64 * row : 64 * row + 64, :]
        square = value * value + SOFTNESS
        inverse = lax.rsqrt(square)
        feature = 0.5 * (value + square * inverse)
        power = jnp.sum(feature * feature, axis=0, keepdims=True) + 1e-6
        norm = lax.rsqrt(power)
        unit = feature * norm
        unit_fake = unit[:, :256]
        direction = weights * (unit_fake - unit[:, 256:])
        inner = jnp.sum(direction * unit_fake, axis=0, keepdims=True)
        slope = 0.5 + 0.5 * (value[:, :256] * inverse[:, :256])
        grad = (direction - unit_fake * inner) * slope * (norm[:, :256] * (2.0 * valid(row - 2)))
        stack = jnp.concatenate([shifted(grad, step).astype(BF16) for step in (1, 0, -1)], axis=0)
        product = dot(second_bwd_ref[...], stack)
        for row_tap in range(3):
            target = row - 2 + row_tap
            if 0 <= target < 6:
                part = product[64 * row_tap : 64 * row_tap + 64]
                acts[target] = part if acts[target] is None else acts[target] + part
    grads = jnp.concatenate(
        [
            (acts[row] * slope_ref[64 * row : 64 * row + 64, :] * valid(row - 1)).astype(BF16)
            for row in range(6)
        ],
        axis=0,
    )
    product = dot(first_bwd_ref[...], grads)
    image_grad = shifted(product[0:16], 1) + product[16:32] + shifted(product[32:48], -1)
    taps = dot(jnp.concatenate(fake, axis=0).astype(BF16), spread_ref[...]).astype(BF16)
    pre = dot(critic_fwd_ref[...], stack_taps(taps, 0))
    slope = 0.6 + 0.4 * (pre * lax.rsqrt(pre * pre + SOFTNESS))
    head = head_ref[...]
    signals = []
    for patch in range(4):
        inside = (first_row + 2 * patch - 2 >= 0) & (first_row + 2 * patch - 2 < 256)
        signals.append((slope[64 * patch : 64 * patch + 64] * (head * -inside.astype(F32))).astype(BF16))
    product = dot(critic_bwd_ref[...], jnp.concatenate(signals, axis=0))
    taps = jnp.concatenate([product[16 * tap : 16 * tap + 16] for tap in range(4)], axis=1)
    high, low = split(taps)
    critic_grad = lax.dot_general(high, spread_ref[...], NT, preferred_element_type=F32) + lax.dot_general(
        low, spread_ref[...], NT, preferred_element_type=F32
    )
    for channel in range(3):
        out_ref[channel] = (
            image_grad[4 * channel : 4 * channel + 4] / LPIPS_SCALE[channel]
            + critic_grad[4 * channel : 4 * channel + 4]
        )


def features(*operands):
    return pl.pallas_call(
        feature_kernel,
        out_shape=jax.ShapeDtypeStruct((3, 4, 256), F32),
        in_specs=[SMEM] + [VMEM] * 14,
        out_specs=VMEM,
        scratch_shapes=[
            pltpu.VMEM((384, 256), F32),
            pltpu.VMEM((640, 512), F32),
            pltpu.VMEM((512, 512), F32),
        ],
        compiler_params=pltpu.CompilerParams(vmem_limit_bytes=16 * 1024 * 1024),
        cost_estimate=pl.CostEstimate(flops=1_000_000_000, bytes_accessed=1_000_000, transcendentals=1_000_000),
        name="features",
    )(*operands)


def finish_kernel(total_ref, conv_ref, head_ref):
    patches = 8 * 128 * 128
    for row in range(24):
        here = total_ref[row // 12 : row // 12 + 1, 128 * (row % 12) : 128 * (row % 12) + 128]
        here = here * (32.0 / 64.0 / patches)
        channel, row_tap = row % 12 // 4, row % 4
        for half in range(2):
            col_tap = 2 * half + row // 12
            conv_ref[channel, row_tap, col_tap : col_tap + 1, :] = here[:, 64 * half : 64 * half + 64]
    head_ref[...] = total_ref[0:1, 1536:1600] * (32.0 / patches)


def finish(total):
    return pl.pallas_call(
        finish_kernel,
        out_shape=[jax.ShapeDtypeStruct((3, 4, 4, 64), F32), jax.ShapeDtypeStruct((1, 64), F32)],
        in_specs=[VMEM],
        out_specs=[VMEM] * 2,
        compiler_params=SMALL,
        name="finish",
    )(total)


def weight_rows(weight):
    moved = jnp.transpose(weight, (1, 2, 3, 0))
    taps = moved.shape[1]
    return jnp.pad(moved, ((0, 0), (0, 4 - taps), (0, 4 - taps), (0, 0))).reshape(48, 64)


def exchange_sum(value, axes, order=None):
    peers = lax.axis_size(axes)
    copies = jnp.broadcast_to(value[None], (peers,) + value.shape)
    groups = None if order is None else [order]
    return jnp.sum(lax.all_to_all(copies, axes, 0, 0, axis_index_groups=groups).astype(F32), axis=0)


def shards(fake, real, vgg_first, vgg_second, lpips_weights, critic_conv, critic_head):
    count = lax.axis_size(ROWS)
    first_row = (lax.axis_index(ROWS) * 4).astype(jnp.int32)[None]
    images = jnp.concatenate([fake, real], axis=0)
    far_pairs = [(k, k + 1) for k in range(15, count - 1, 16)]
    whole = images.astype(F32)
    under = lax.ppermute(whole, ROWS, [(b, b + MIDDLE) for a, b in far_pairs])
    upper = lax.ppermute(whole, ROWS, [(a, b + MIDDLE) for a, b in far_pairs])
    critic_rows = weight_rows(critic_conv)
    spread, critic_fwd, head = critic_weights(critic_rows, critic_head[None])
    previous = lax.ppermute(images, ROWS, [(k, k + 1) for k in range(count - 1) if k % 16 < 15])
    following = lax.ppermute(whole, ROWS, [(k + 1, k) for k in range(count - 1) if k % 16 < 15])
    early = lax.ppermute(upper, ("zh",) + ROWS, [(b + MIDDLE, b) for a, b in far_pairs])
    rest = [(count + a, count + b) for a, b in far_pairs]
    for base in (0, count):
        rest += [(base + b + MIDDLE, base + a) for a, b in far_pairs]
    sums = critic(first_row, under, upper, previous, images, spread, critic_fwd, head)
    plane = exchange_sum(sums.astype(jnp.float16), PLANE, PLANE_ORDER)
    plane, first, second, again = lax.optimization_barrier(
        (plane, weight_rows(vgg_first), jnp.transpose(vgg_second, (2, 3, 0, 1)), critic_rows)
    )
    *weights, copied = feature_weights(first_row, first, second, again, following, early, under, images)
    late = lax.ppermute(copied, ("zh",) + ROWS, rest)
    total = exchange_sum((plane * (1.0 / 32.0)).astype(jnp.float16), COLUMN, COLUMN_ORDER)
    grad_image = features(
        first_row, *weights, previous, images, following, early, late, lpips_weights[:, None], spread, critic_fwd, head
    )
    conv_grad, head_grad = finish(total)
    return grad_image[None], jnp.transpose(conv_grad, (3, 0, 1, 2)), head_grad[0]


def solution(mesh):
    wide = Mesh(mesh.devices.reshape(2, 4, 4, 8, 2), ("zh", "y", "x", "zl", "c"))
    return jax.shard_map(
        shards,
        mesh=wide,
        in_specs=(P(DP, None, ROWS, None), P(DP, None, ROWS, None), P(), P(), P(), P(), P()),
        out_specs=(P(DP, None, ROWS, None), P(), P()),
        check_vma=False,
    )
```

```python
import functools

import jax
import jax.numpy as jnp
from jax import lax
from jax.experimental import pallas as pl
from jax.experimental.pallas import tpu as pltpu
from jax.sharding import Mesh, PartitionSpec as P

LPIPS_SHIFT = (-0.03, -0.088, -0.188)
LPIPS_SCALE = (0.458, 0.448, 0.45)
SOFTNESS = 0.04
ROWS = ("x", "zl", "c")
DP = ("zh", "y")
PLANE = ("y", "x", "c")
COLUMN = ("zh", "zl")
MIDDLE = 9
PLANE_ORDER = [21, 0, 1, 2, 3, 6, 7, 8, 9, 24, 25, 4, 5, 10, 11, 14, 15, 16, 17, 26, 27, 30, 31, 12, 13, 18, 19, 22, 23, 28, 29, 20]
COLUMN_ORDER = [10, 8, 7, 6, 9, 5, 4, 3, 2, 11, 12, 13, 14, 1, 15, 0]
F32 = jnp.float32
BF16 = jnp.bfloat16
VMEM = pl.BlockSpec(memory_space=pltpu.VMEM)
SMEM = pl.BlockSpec(memory_space=pltpu.SMEM)
TN = (((0,), (0,)), ((), ()))
NT = (((1,), (1,)), ((), ()))
SMALL = pltpu.CompilerParams(vmem_limit_bytes=8 * 1024 * 1024)


def iota(shape, dim):
    return lax.broadcasted_iota(jnp.int32, shape, dim)


def dot(lhs, rhs):
    return jnp.dot(lhs, rhs, preferred_element_type=F32)


def split(value):
    high = value.astype(BF16)
    return high, (value - high.astype(F32)).astype(BF16)


def tap_index(m):
    return m >> 4, (m >> 2) & 3, m & 3


def block_index(k):
    tap = (k >= 48).astype(jnp.int32) + (k >= 96).astype(jnp.int32) + (k >= 144).astype(jnp.int32)
    rest = k - 48 * tap
    return tap, rest >> 4, rest & 15


def expand(weight, width, first_row):
    channel, row_tap, col_tap = tap_index(iota((48, width), 0))
    block_tap, block_channel, block_row = block_index(iota((48, width), 1))
    chosen = (channel == block_channel) & (col_tap == block_tap) & (block_row == first_row + row_tap)
    return lax.dot_general(
        weight, chosen.astype(F32).astype(BF16), TN, preferred_element_type=F32
    ).astype(BF16)


def critic_weights_kernel(critic_ref, head_ref, spread_ref, fwd_ref, column_ref):
    column = iota((256, 512), 0)
    place = iota((256, 512), 1)
    spread_ref[...] = (column == 2 * (place & 127) + (place >> 7) - 1).astype(F32).astype(BF16)
    critic = critic_ref[...]
    for patch in range(4):
        fwd_ref[64 * patch : 64 * patch + 64, :] = expand(critic, 192, 1 + 2 * patch)
    diagonal = iota((64, 64), 0) == iota((64, 64), 1)
    column_ref[...] = jnp.sum(jnp.where(diagonal, head_ref[...], 0.0), axis=1, keepdims=True)


def critic_weights(critic, head):
    return pl.pallas_call(
        critic_weights_kernel,
        out_shape=[
            jax.ShapeDtypeStruct((256, 512), BF16),
            jax.ShapeDtypeStruct((256, 192), BF16),
            jax.ShapeDtypeStruct((64, 1), F32),
        ],
        in_specs=[VMEM] * 2,
        out_specs=[VMEM] * 3,
        compiler_params=SMALL,
        name="critic_weights",
    )(critic, head)


def feature_weights_kernel(row_ref, first_ref, second_ref, critic_ref, next_ref, early_ref, under_ref, image_ref,
                           critic_bwd_ref, first_fwd_ref, first_bwd_ref,
                           second_fwd_ref, second_bwd_ref, copy_ref):
    between = (row_ref[0] // 4 & 15) == MIDDLE
    copy_ref[...] = jnp.where(between, under_ref[...], image_ref[...].astype(F32)).astype(BF16)
    critic = critic_ref[...]
    first = first_ref[...]
    for row in range(10):
        first_fwd_ref[64 * row : 64 * row + 64, :] = expand(first, 144, row)

    def gather(weight, shift):
        row = iota((64, 48), 0)
        channel, row_tap, col_tap = tap_index(iota((64, 48), 1))
        inner = row & 15
        chosen = (row >> 4 == col_tap) & (inner >> 2 == channel) & ((inner & 3) + shift == row_tap)
        return dot(chosen.astype(F32).astype(BF16), weight).astype(BF16)

    critic_bwd_ref[...] = jnp.concatenate([gather(critic, 3 - 2 * patch) for patch in range(4)], axis=1)
    first_bwd_ref[...] = jnp.concatenate([gather(first, 2 - row)[:48] for row in range(6)], axis=1)
    for row_tap in range(3):
        second_fwd_ref[64 * row_tap : 64 * row_tap + 64, :] = jnp.concatenate(
            [second_ref[row_tap, col_tap] for col_tap in range(3)], axis=1
        )
        second_bwd_ref[64 * row_tap : 64 * row_tap + 64, :] = jnp.concatenate(
            [second_ref[row_tap, col_tap].astype(F32).T.astype(BF16) for col_tap in range(3)], axis=1
        )


def feature_weights(*operands):
    shapes = [(64, 256), (640, 144), (48, 384), (192, 192), (192, 192), (2, 3, 4, 256)]
    return pl.pallas_call(
        feature_weights_kernel,
        out_shape=[jax.ShapeDtypeStruct(shape, BF16) for shape in shapes],
        in_specs=[SMEM] + [VMEM] * 7,
        out_specs=[VMEM] * len(shapes),
        compiler_params=SMALL,
        cost_estimate=pl.CostEstimate(flops=20_000_000_000, bytes_accessed=1_000_000, transcendentals=0),
        name="feature_weights",
    )(*operands)


def stack_taps(taps, image):
    return jnp.concatenate(
        [taps[48 * image : 48 * image + 48, 128 * tap : 128 * tap + 128] for tap in range(4)], axis=0
    )


def critic_kernel(row_ref, under_ref, upper_ref, previous_ref, image_ref, spread_ref, weight_ref, head_ref, sums_ref):
    index = row_ref[0] // 4
    last = index == 63
    between = ((index & 15) == MIDDLE) & (index > 15)
    near = (index & 15) != 0
    shares = (
        (near.astype(F32), (between | last).astype(F32)),
        ((near | (index == 0)).astype(F32), between.astype(F32)),
    )
    blank = jnp.zeros((8, 256), F32)
    rows = []
    for image in range(2):
        for channel in range(3):
            rows += [previous_ref[image, channel].astype(F32), image_ref[image, channel].astype(F32), blank]
    for image in range(2):
        for channel in range(3):
            upper = jnp.where(last, image_ref[image, channel].astype(F32), upper_ref[image, channel])
            rows += [upper, under_ref[image, channel], blank]
    taps = dot(jnp.concatenate(rows, axis=0).astype(BF16), spread_ref[...]).astype(BF16)
    windows = jnp.concatenate([stack_taps(taps, place) for place in range(4)], axis=1)
    pre = dot(weight_ref[0:128, :], windows)
    head = head_ref[...]
    square = pre * pre + SOFTNESS
    inverse = lax.rsqrt(square)
    hidden = 0.6 * pre + 0.4 * (square * inverse)
    slope = 0.6 + 0.4 * (pre * inverse)
    lane = iota((1, 512), 1)
    signals = []
    total = None
    for patch in range(2):
        part = hidden[64 * patch : 64 * patch + 64]
        logit = jnp.sum(head * part, axis=0, keepdims=True)
        sign = jnp.where(
            (lane & 128) == 0, jnp.where(logit > -1.0, 1.0, 0.0), jnp.where(logit < 1.0, -1.0, 0.0)
        ) * jnp.where(lane < 256, shares[patch][0], shares[patch][1])
        signals.append(slope[64 * patch : 64 * patch + 64] * (head * sign))
        total = part * sign if total is None else total + part * sign
    high, low = split(jnp.concatenate(signals + [total], axis=0))
    windows = jnp.concatenate([windows, jnp.ones((16, 512), BF16)], axis=0)
    grads = lax.dot_general(windows, high, NT, preferred_element_type=F32) + lax.dot_general(
        windows, low, NT, preferred_element_type=F32
    )
    rows = []
    for block in range(12):
        here = grads[16 * block : 16 * block + 16]
        rows.append(here[1:5, :64] + here[3:7, 64:128])
    packed = 64.0 * jnp.concatenate(
        [jnp.concatenate(rows[:6], axis=0), jnp.concatenate(rows[6:], axis=0)], axis=1
    )
    for row in range(24):
        sums_ref[row // 12 : row // 12 + 1, 128 * (row % 12) : 128 * (row % 12) + 128] = packed[row : row + 1]
    head_sum = jnp.concatenate([grads[192:194, 128:192], jnp.zeros((2, 64), F32)], axis=1)
    sums_ref[:, 1536:1664] = head_sum


def critic(*operands):
    return pl.pallas_call(
        critic_kernel,
        out_shape=jax.ShapeDtypeStruct((2, 1664), F32),
        in_specs=[SMEM] + [VMEM] * 7,
        out_specs=VMEM,
        compiler_params=SMALL,
        name="critic",
    )(*operands)


def shifted(value, step):
    if step == 0:
        return value
    zero = jnp.zeros(value.shape[:1] + (1,), value.dtype)
    parts = []
    for start in range(0, value.shape[1], 256):
        here = value[:, start : start + 256]
        if step > 0:
            parts.append(jnp.concatenate([here[:, 1:], zero], axis=1))
        else:
            parts.append(jnp.concatenate([zero, here[:, :-1]], axis=1))
    return parts[0] if len(parts) == 1 else jnp.concatenate(parts, axis=1)


def feature_kernel(row_ref, critic_bwd_ref, first_fwd_ref, first_bwd_ref, second_fwd_ref, second_bwd_ref,
                   previous_ref, image_ref, next_ref, early_ref, late_ref, lpips_ref, spread_ref, critic_fwd_ref, head_ref,
                   out_ref, slope_ref, pre_ref, act_ref):
    first_row = row_ref[0]
    place = first_row // 4 & 15

    def valid(row):
        return ((first_row + row >= 0) & (first_row + row < 256)).astype(F32)

    line = iota((16, 256), 0) + (first_row - 4)
    inside = ((line >= 0) & (line < 256)).astype(F32)
    images = []
    fake = []
    for image in range(2):
        parts = []
        for channel in range(3):
            far = late_ref[image, channel].astype(F32)
            above = jnp.where(place == 0, early_ref[image, channel] + far, previous_ref[image, channel].astype(F32))
            below = jnp.where(place == 15, far, next_ref[image, channel])
            here = jnp.concatenate(
                [above, image_ref[image, channel].astype(F32), below, jnp.zeros_like(far)], axis=0
            )
            if image == 0:
                fake.append(here)
            parts.append((here - LPIPS_SHIFT[channel]) / LPIPS_SCALE[channel] * inside)
        images.append(jnp.concatenate(parts, axis=0))
    scaled = jnp.concatenate(images, axis=1)
    windows = jnp.concatenate([shifted(scaled, step).astype(BF16) for step in (-1, 0, 1)], axis=0)
    pre_ref[...] = dot(first_fwd_ref[...], windows)
    for row in range(10):
        value = pre_ref[64 * row : 64 * row + 64, :]
        square = value * value + SOFTNESS
        inverse = lax.rsqrt(square)
        if 2 <= row < 8:
            slope_ref[64 * row - 128 : 64 * row - 64, :] = 0.5 + 0.5 * (value * inverse)[:, :256]
        act = (value + square * inverse) * (0.5 * valid(row - 3))
        stack = jnp.concatenate([shifted(act, step).astype(BF16) for step in (-1, 0, 1)], axis=0)
        product = dot(second_fwd_ref[...], stack)
        for row_tap in range(3):
            target = row - row_tap
            if 0 <= target < 8:
                part = product[64 * row_tap : 64 * row_tap + 64]
                if row_tap == 0:
                    act_ref[64 * target : 64 * target + 64, :] = part
                else:
                    act_ref[64 * target : 64 * target + 64, :] += part
    weights = lpips_ref[...]
    acts = [None] * 6
    for row in range(8):
        value = act_ref[64 * row : 64 * row + 64, :]
        square = value * value + SOFTNESS
        inverse = lax.rsqrt(square)
        feature = 0.5 * (value + square * inverse)
        power = jnp.sum(feature * feature, axis=0, keepdims=True) + 1e-6
        norm = lax.rsqrt(power)
        unit = feature * norm
        unit_fake = unit[:, :256]
        direction = weights * (unit_fake - unit[:, 256:])
        inner = jnp.sum(direction * unit_fake, axis=0, keepdims=True)
        slope = 0.5 + 0.5 * (value[:, :256] * inverse[:, :256])
        grad = (direction - unit_fake * inner) * slope * (norm[:, :256] * (2.0 * valid(row - 2)))
        stack = jnp.concatenate([shifted(grad, step).astype(BF16) for step in (1, 0, -1)], axis=0)
        product = dot(second_bwd_ref[...], stack)
        for row_tap in range(3):
            target = row - 2 + row_tap
            if 0 <= target < 6:
                part = product[64 * row_tap : 64 * row_tap + 64]
                acts[target] = part if acts[target] is None else acts[target] + part
    grads = jnp.concatenate(
        [
            (acts[row] * slope_ref[64 * row : 64 * row + 64, :] * valid(row - 1)).astype(BF16)
            for row in range(6)
        ],
        axis=0,
    )
    product = dot(first_bwd_ref[...], grads)
    image_grad = shifted(product[0:16], 1) + product[16:32] + shifted(product[32:48], -1)
    taps = dot(jnp.concatenate(fake, axis=0).astype(BF16), spread_ref[...]).astype(BF16)
    pre = dot(critic_fwd_ref[...], stack_taps(taps, 0))
    slope = 0.6 + 0.4 * (pre * lax.rsqrt(pre * pre + SOFTNESS))
    head = head_ref[...]
    signals = []
    for patch in range(4):
        inside = (first_row + 2 * patch - 2 >= 0) & (first_row + 2 * patch - 2 < 256)
        signals.append((slope[64 * patch : 64 * patch + 64] * (head * -inside.astype(F32))).astype(BF16))
    product = dot(critic_bwd_ref[...], jnp.concatenate(signals, axis=0))
    taps = jnp.concatenate([product[16 * tap : 16 * tap + 16] for tap in range(4)], axis=1)
    high, low = split(taps)
    critic_grad = lax.dot_general(high, spread_ref[...], NT, preferred_element_type=F32) + lax.dot_general(
        low, spread_ref[...], NT, preferred_element_type=F32
    )
    for channel in range(3):
        out_ref[channel] = (
            image_grad[4 * channel : 4 * channel + 4] / LPIPS_SCALE[channel]
            + critic_grad[4 * channel : 4 * channel + 4]
        )


def features(*operands):
    return pl.pallas_call(
        feature_kernel,
        out_shape=jax.ShapeDtypeStruct((3, 4, 256), F32),
        in_specs=[SMEM] + [VMEM] * 14,
        out_specs=VMEM,
        scratch_shapes=[
            pltpu.VMEM((384, 256), F32),
            pltpu.VMEM((640, 512), F32),
            pltpu.VMEM((512, 512), F32),
        ],
        compiler_params=pltpu.CompilerParams(vmem_limit_bytes=16 * 1024 * 1024),
        cost_estimate=pl.CostEstimate(flops=1_000_000_000, bytes_accessed=1_000_000, transcendentals=1_000_000),
        name="features",
    )(*operands)


def finish_kernel(total_ref, conv_ref, head_ref):
    patches = 8 * 128 * 128
    for row in range(24):
        here = total_ref[row // 12 : row // 12 + 1, 128 * (row % 12) : 128 * (row % 12) + 128]
        here = here * (32.0 / 64.0 / patches)
        channel, row_tap = row % 12 // 4, row % 4
        for half in range(2):
            col_tap = 2 * half + row // 12
            conv_ref[channel, row_tap, col_tap : col_tap + 1, :] = here[:, 64 * half : 64 * half + 64]
    head_ref[...] = total_ref[0:1, 1536:1600] * (32.0 / patches)


def finish(total):
    return pl.pallas_call(
        finish_kernel,
        out_shape=[jax.ShapeDtypeStruct((3, 4, 4, 64), F32), jax.ShapeDtypeStruct((1, 64), F32)],
        in_specs=[VMEM],
        out_specs=[VMEM] * 2,
        compiler_params=SMALL,
        name="finish",
    )(total)


def weight_rows(weight):
    moved = jnp.transpose(weight, (1, 2, 3, 0))
    taps = moved.shape[1]
    return jnp.pad(moved, ((0, 0), (0, 4 - taps), (0, 4 - taps), (0, 0))).reshape(48, 64)


def exchange_sum(value, axes, order=None):
    peers = lax.axis_size(axes)
    copies = jnp.broadcast_to(value[None], (peers,) + value.shape)
    groups = None if order is None else [order]
    return jnp.sum(lax.all_to_all(copies, axes, 0, 0, axis_index_groups=groups).astype(F32), axis=0)


def shards(fake, real, vgg_first, vgg_second, lpips_weights, critic_conv, critic_head):
    count = lax.axis_size(ROWS)
    first_row = (lax.axis_index(ROWS) * 4).astype(jnp.int32)[None]
    images = jnp.concatenate([fake, real], axis=0)
    far_pairs = [(k, k + 1) for k in range(15, count - 1, 16)]
    whole = images.astype(F32)
    under = lax.ppermute(whole, ROWS, [(b, b + MIDDLE) for a, b in far_pairs])
    upper = lax.ppermute(whole, ROWS, [(a, b + MIDDLE) for a, b in far_pairs])
    critic_rows = weight_rows(critic_conv)
    spread, critic_fwd, head = critic_weights(critic_rows, critic_head[None])
    previous = lax.ppermute(images, ROWS, [(k, k + 1) for k in range(count - 1) if k % 16 < 15])
    following = lax.ppermute(whole, ROWS, [(k + 1, k) for k in range(count - 1) if k % 16 < 15])
    early = lax.ppermute(upper, ("zh",) + ROWS, [(b + MIDDLE, b) for a, b in far_pairs])
    rest = [(count + a, count + b) for a, b in far_pairs]
    for base in (0, count):
        rest += [(base + b + MIDDLE, base + a) for a, b in far_pairs]
    sums = critic(first_row, under, upper, previous, images, spread, critic_fwd, head)
    plane = exchange_sum(sums.astype(jnp.float16), PLANE, PLANE_ORDER)
    plane, first, second, again = lax.optimization_barrier(
        (plane, weight_rows(vgg_first), jnp.transpose(vgg_second, (2, 3, 0, 1)), critic_rows)
    )
    *weights, copied = feature_weights(first_row, first, second, again, following, early, under, images)
    late = lax.ppermute(copied, ("zh",) + ROWS, rest)
    total = exchange_sum((plane * (1.0 / 32.0)).astype(jnp.float16), COLUMN, COLUMN_ORDER)
    grad_image = features(
        first_row, *weights, previous, images, following, early, late, lpips_weights[:, None], spread, critic_fwd, head
    )
    conv_grad, head_grad = finish(total)
    return grad_image[None], jnp.transpose(conv_grad, (3, 0, 1, 2)), head_grad[0]


def solution(mesh):
    wide = Mesh(mesh.devices.reshape(2, 4, 4, 8, 2), ("zh", "y", "x", "zl", "c"))
    return jax.shard_map(
        shards,
        mesh=wide,
        in_specs=(P(DP, None, ROWS, None), P(DP, None, ROWS, None), P(), P(), P(), P(), P()),
        out_specs=(P(DP, None, ROWS, None), P(), P()),
        check_vma=False,
    )
```

```python
import functools

import jax
import jax.numpy as jnp
from jax import lax
from jax.experimental import pallas as pl
from jax.experimental.pallas import tpu as pltpu
from jax.sharding import Mesh, PartitionSpec as P

LPIPS_SHIFT = (-0.03, -0.088, -0.188)
LPIPS_SCALE = (0.458, 0.448, 0.45)
SOFTNESS = 0.04
ROWS = ("x", "zl", "c")
DP = ("zh", "y")
PLANE = ("y", "x", "c")
COLUMN = ("zh", "zl")
MIDDLE = 9
PLANE_ORDER = [21, 0, 1, 2, 3, 6, 7, 8, 9, 24, 25, 4, 5, 10, 11, 14, 15, 16, 17, 26, 27, 30, 31, 12, 13, 18, 19, 22, 23, 28, 29, 20]
COLUMN_ORDER = [11, 0, 1, 2, 3, 15, 4, 14, 5, 13, 6, 12, 7, 10, 8, 9]
F32 = jnp.float32
BF16 = jnp.bfloat16
VMEM = pl.BlockSpec(memory_space=pltpu.VMEM)
SMEM = pl.BlockSpec(memory_space=pltpu.SMEM)
TN = (((0,), (0,)), ((), ()))
NT = (((1,), (1,)), ((), ()))
SMALL = pltpu.CompilerParams(vmem_limit_bytes=8 * 1024 * 1024)


def iota(shape, dim):
    return lax.broadcasted_iota(jnp.int32, shape, dim)


def dot(lhs, rhs):
    return jnp.dot(lhs, rhs, preferred_element_type=F32)


def split(value):
    high = value.astype(BF16)
    return high, (value - high.astype(F32)).astype(BF16)


def tap_index(m):
    return m >> 4, (m >> 2) & 3, m & 3


def block_index(k):
    tap = (k >= 48).astype(jnp.int32) + (k >= 96).astype(jnp.int32) + (k >= 144).astype(jnp.int32)
    rest = k - 48 * tap
    return tap, rest >> 4, rest & 15


def expand(weight, width, first_row):
    channel, row_tap, col_tap = tap_index(iota((48, width), 0))
    block_tap, block_channel, block_row = block_index(iota((48, width), 1))
    chosen = (channel == block_channel) & (col_tap == block_tap) & (block_row == first_row + row_tap)
    return lax.dot_general(
        weight, chosen.astype(F32).astype(BF16), TN, preferred_element_type=F32
    ).astype(BF16)


def critic_weights_kernel(critic_ref, head_ref, spread_ref, fwd_ref, column_ref):
    column = iota((256, 512), 0)
    place = iota((256, 512), 1)
    spread_ref[...] = (column == 2 * (place & 127) + (place >> 7) - 1).astype(F32).astype(BF16)
    critic = critic_ref[...]
    for patch in range(4):
        fwd_ref[64 * patch : 64 * patch + 64, :] = expand(critic, 192, 1 + 2 * patch)
    diagonal = iota((64, 64), 0) == iota((64, 64), 1)
    column_ref[...] = jnp.sum(jnp.where(diagonal, head_ref[...], 0.0), axis=1, keepdims=True)


def critic_weights(critic, head):
    return pl.pallas_call(
        critic_weights_kernel,
        out_shape=[
            jax.ShapeDtypeStruct((256, 512), BF16),
            jax.ShapeDtypeStruct((256, 192), BF16),
            jax.ShapeDtypeStruct((64, 1), F32),
        ],
        in_specs=[VMEM] * 2,
        out_specs=[VMEM] * 3,
        compiler_params=SMALL,
        name="critic_weights",
    )(critic, head)


def feature_weights_kernel(row_ref, first_ref, second_ref, critic_ref, next_ref, early_ref, under_ref, image_ref,
                           critic_bwd_ref, first_fwd_ref, first_bwd_ref,
                           second_fwd_ref, second_bwd_ref, copy_ref):
    between = (row_ref[0] // 4 & 15) == MIDDLE
    copy_ref[...] = jnp.where(between, under_ref[...], image_ref[...].astype(F32)).astype(BF16)
    critic = critic_ref[...]
    first = first_ref[...]
    for row in range(10):
        first_fwd_ref[64 * row : 64 * row + 64, :] = expand(first, 144, row)

    def gather(weight, shift):
        row = iota((64, 48), 0)
        channel, row_tap, col_tap = tap_index(iota((64, 48), 1))
        inner = row & 15
        chosen = (row >> 4 == col_tap) & (inner >> 2 == channel) & ((inner & 3) + shift == row_tap)
        return dot(chosen.astype(F32).astype(BF16), weight).astype(BF16)

    critic_bwd_ref[...] = jnp.concatenate([gather(critic, 3 - 2 * patch) for patch in range(4)], axis=1)
    first_bwd_ref[...] = jnp.concatenate([gather(first, 2 - row)[:48] for row in range(6)], axis=1)
    for row_tap in range(3):
        second_fwd_ref[64 * row_tap : 64 * row_tap + 64, :] = jnp.concatenate(
            [second_ref[row_tap, col_tap] for col_tap in range(3)], axis=1
        )
        second_bwd_ref[64 * row_tap : 64 * row_tap + 64, :] = jnp.concatenate(
            [second_ref[row_tap, col_tap].astype(F32).T.astype(BF16) for col_tap in range(3)], axis=1
        )


def feature_weights(*operands):
    shapes = [(64, 256), (640, 144), (48, 384), (192, 192), (192, 192), (2, 3, 4, 256)]
    return pl.pallas_call(
        feature_weights_kernel,
        out_shape=[jax.ShapeDtypeStruct(shape, BF16) for shape in shapes],
        in_specs=[SMEM] + [VMEM] * 7,
        out_specs=[VMEM] * len(shapes),
        compiler_params=SMALL,
        cost_estimate=pl.CostEstimate(flops=20_000_000_000, bytes_accessed=1_000_000, transcendentals=0),
        name="feature_weights",
    )(*operands)


def stack_taps(taps, image):
    return jnp.concatenate(
        [taps[48 * image : 48 * image + 48, 128 * tap : 128 * tap + 128] for tap in range(4)], axis=0
    )


def critic_kernel(row_ref, under_ref, upper_ref, previous_ref, image_ref, spread_ref, weight_ref, head_ref, sums_ref):
    index = row_ref[0] // 4
    last = index == 63
    between = ((index & 15) == MIDDLE) & (index > 15)
    near = (index & 15) != 0
    shares = (
        (near.astype(F32), (between | last).astype(F32)),
        ((near | (index == 0)).astype(F32), between.astype(F32)),
    )
    blank = jnp.zeros((8, 256), F32)
    rows = []
    for image in range(2):
        for channel in range(3):
            rows += [previous_ref[image, channel].astype(F32), image_ref[image, channel].astype(F32), blank]
    for image in range(2):
        for channel in range(3):
            upper = jnp.where(last, image_ref[image, channel].astype(F32), upper_ref[image, channel])
            rows += [upper, under_ref[image, channel], blank]
    taps = dot(jnp.concatenate(rows, axis=0).astype(BF16), spread_ref[...]).astype(BF16)
    windows = jnp.concatenate([stack_taps(taps, place) for place in range(4)], axis=1)
    pre = dot(weight_ref[0:128, :], windows)
    head = head_ref[...]
    square = pre * pre + SOFTNESS
    inverse = lax.rsqrt(square)
    hidden = 0.6 * pre + 0.4 * (square * inverse)
    slope = 0.6 + 0.4 * (pre * inverse)
    lane = iota((1, 512), 1)
    signals = []
    total = None
    for patch in range(2):
        part = hidden[64 * patch : 64 * patch + 64]
        logit = jnp.sum(head * part, axis=0, keepdims=True)
        sign = jnp.where(
            (lane & 128) == 0, jnp.where(logit > -1.0, 1.0, 0.0), jnp.where(logit < 1.0, -1.0, 0.0)
        ) * jnp.where(lane < 256, shares[patch][0], shares[patch][1])
        signals.append(slope[64 * patch : 64 * patch + 64] * (head * sign))
        total = part * sign if total is None else total + part * sign
    high, low = split(jnp.concatenate(signals + [total], axis=0))
    windows = jnp.concatenate([windows, jnp.ones((16, 512), BF16)], axis=0)
    grads = lax.dot_general(windows, high, NT, preferred_element_type=F32) + lax.dot_general(
        windows, low, NT, preferred_element_type=F32
    )
    rows = []
    for block in range(12):
        here = grads[16 * block : 16 * block + 16]
        rows.append(here[1:5, :64] + here[3:7, 64:128])
    packed = 64.0 * jnp.concatenate(
        [jnp.concatenate(rows[:6], axis=0), jnp.concatenate(rows[6:], axis=0)], axis=1
    )
    for row in range(24):
        sums_ref[row // 12 : row // 12 + 1, 128 * (row % 12) : 128 * (row % 12) + 128] = packed[row : row + 1]
    head_sum = jnp.concatenate([grads[192:194, 128:192], jnp.zeros((2, 64), F32)], axis=1)
    sums_ref[:, 1536:1664] = head_sum


def critic(*operands):
    return pl.pallas_call(
        critic_kernel,
        out_shape=jax.ShapeDtypeStruct((2, 1664), F32),
        in_specs=[SMEM] + [VMEM] * 7,
        out_specs=VMEM,
        compiler_params=SMALL,
        name="critic",
    )(*operands)


def shifted(value, step):
    if step == 0:
        return value
    zero = jnp.zeros(value.shape[:1] + (1,), value.dtype)
    parts = []
    for start in range(0, value.shape[1], 256):
        here = value[:, start : start + 256]
        if step > 0:
            parts.append(jnp.concatenate([here[:, 1:], zero], axis=1))
        else:
            parts.append(jnp.concatenate([zero, here[:, :-1]], axis=1))
    return parts[0] if len(parts) == 1 else jnp.concatenate(parts, axis=1)


def feature_kernel(row_ref, critic_bwd_ref, first_fwd_ref, first_bwd_ref, second_fwd_ref, second_bwd_ref,
                   previous_ref, image_ref, next_ref, early_ref, late_ref, lpips_ref, spread_ref, critic_fwd_ref, head_ref,
                   out_ref, slope_ref, pre_ref, act_ref):
    first_row = row_ref[0]
    place = first_row // 4 & 15

    def valid(row):
        return ((first_row + row >= 0) & (first_row + row < 256)).astype(F32)

    line = iota((16, 256), 0) + (first_row - 4)
    inside = ((line >= 0) & (line < 256)).astype(F32)
    images = []
    fake = []
    for image in range(2):
        parts = []
        for channel in range(3):
            far = late_ref[image, channel].astype(F32)
            above = jnp.where(place == 0, early_ref[image, channel] + far, previous_ref[image, channel].astype(F32))
            below = jnp.where(place == 15, far, next_ref[image, channel])
            here = jnp.concatenate(
                [above, image_ref[image, channel].astype(F32), below, jnp.zeros_like(far)], axis=0
            )
            if image == 0:
                fake.append(here)
            parts.append((here - LPIPS_SHIFT[channel]) / LPIPS_SCALE[channel] * inside)
        images.append(jnp.concatenate(parts, axis=0))
    scaled = jnp.concatenate(images, axis=1)
    windows = jnp.concatenate([shifted(scaled, step).astype(BF16) for step in (-1, 0, 1)], axis=0)
    pre_ref[...] = dot(first_fwd_ref[...], windows)
    for row in range(10):
        value = pre_ref[64 * row : 64 * row + 64, :]
        square = value * value + SOFTNESS
        inverse = lax.rsqrt(square)
        if 2 <= row < 8:
            slope_ref[64 * row - 128 : 64 * row - 64, :] = 0.5 + 0.5 * (value * inverse)[:, :256]
        act = (value + square * inverse) * (0.5 * valid(row - 3))
        stack = jnp.concatenate([shifted(act, step).astype(BF16) for step in (-1, 0, 1)], axis=0)
        product = dot(second_fwd_ref[...], stack)
        for row_tap in range(3):
            target = row - row_tap
            if 0 <= target < 8:
                part = product[64 * row_tap : 64 * row_tap + 64]
                if row_tap == 0:
                    act_ref[64 * target : 64 * target + 64, :] = part
                else:
                    act_ref[64 * target : 64 * target + 64, :] += part
    weights = lpips_ref[...]
    acts = [None] * 6
    for row in range(8):
        value = act_ref[64 * row : 64 * row + 64, :]
        square = value * value + SOFTNESS
        inverse = lax.rsqrt(square)
        feature = 0.5 * (value + square * inverse)
        power = jnp.sum(feature * feature, axis=0, keepdims=True) + 1e-6
        norm = lax.rsqrt(power)
        unit = feature * norm
        unit_fake = unit[:, :256]
        direction = weights * (unit_fake - unit[:, 256:])
        inner = jnp.sum(direction * unit_fake, axis=0, keepdims=True)
        slope = 0.5 + 0.5 * (value[:, :256] * inverse[:, :256])
        grad = (direction - unit_fake * inner) * slope * (norm[:, :256] * (2.0 * valid(row - 2)))
        stack = jnp.concatenate([shifted(grad, step).astype(BF16) for step in (1, 0, -1)], axis=0)
        product = dot(second_bwd_ref[...], stack)
        for row_tap in range(3):
            target = row - 2 + row_tap
            if 0 <= target < 6:
                part = product[64 * row_tap : 64 * row_tap + 64]
                acts[target] = part if acts[target] is None else acts[target] + part
    grads = jnp.concatenate(
        [
            (acts[row] * slope_ref[64 * row : 64 * row + 64, :] * valid(row - 1)).astype(BF16)
            for row in range(6)
        ],
        axis=0,
    )
    product = dot(first_bwd_ref[...], grads)
    image_grad = shifted(product[0:16], 1) + product[16:32] + shifted(product[32:48], -1)
    taps = dot(jnp.concatenate(fake, axis=0).astype(BF16), spread_ref[...]).astype(BF16)
    pre = dot(critic_fwd_ref[...], stack_taps(taps, 0))
    slope = 0.6 + 0.4 * (pre * lax.rsqrt(pre * pre + SOFTNESS))
    head = head_ref[...]
    signals = []
    for patch in range(4):
        inside = (first_row + 2 * patch - 2 >= 0) & (first_row + 2 * patch - 2 < 256)
        signals.append((slope[64 * patch : 64 * patch + 64] * (head * -inside.astype(F32))).astype(BF16))
    product = dot(critic_bwd_ref[...], jnp.concatenate(signals, axis=0))
    taps = jnp.concatenate([product[16 * tap : 16 * tap + 16] for tap in range(4)], axis=1)
    high, low = split(taps)
    critic_grad = lax.dot_general(high, spread_ref[...], NT, preferred_element_type=F32) + lax.dot_general(
        low, spread_ref[...], NT, preferred_element_type=F32
    )
    for channel in range(3):
        out_ref[channel] = (
            image_grad[4 * channel : 4 * channel + 4] / LPIPS_SCALE[channel]
            + critic_grad[4 * channel : 4 * channel + 4]
        )


def features(*operands):
    return pl.pallas_call(
        feature_kernel,
        out_shape=jax.ShapeDtypeStruct((3, 4, 256), F32),
        in_specs=[SMEM] + [VMEM] * 14,
        out_specs=VMEM,
        scratch_shapes=[
            pltpu.VMEM((384, 256), F32),
            pltpu.VMEM((640, 512), F32),
            pltpu.VMEM((512, 512), F32),
        ],
        compiler_params=pltpu.CompilerParams(vmem_limit_bytes=16 * 1024 * 1024),
        cost_estimate=pl.CostEstimate(flops=1_000_000_000, bytes_accessed=1_000_000, transcendentals=1_000_000),
        name="features",
    )(*operands)


def finish_kernel(total_ref, conv_ref, head_ref):
    patches = 8 * 128 * 128
    for row in range(24):
        here = total_ref[row // 12 : row // 12 + 1, 128 * (row % 12) : 128 * (row % 12) + 128]
        here = here * (32.0 / 64.0 / patches)
        channel, row_tap = row % 12 // 4, row % 4
        for half in range(2):
            col_tap = 2 * half + row // 12
            conv_ref[channel, row_tap, col_tap : col_tap + 1, :] = here[:, 64 * half : 64 * half + 64]
    head_ref[...] = total_ref[0:1, 1536:1600] * (32.0 / patches)


def finish(total):
    return pl.pallas_call(
        finish_kernel,
        out_shape=[jax.ShapeDtypeStruct((3, 4, 4, 64), F32), jax.ShapeDtypeStruct((1, 64), F32)],
        in_specs=[VMEM],
        out_specs=[VMEM] * 2,
        compiler_params=SMALL,
        name="finish",
    )(total)


def weight_rows(weight):
    moved = jnp.transpose(weight, (1, 2, 3, 0))
    taps = moved.shape[1]
    return jnp.pad(moved, ((0, 0), (0, 4 - taps), (0, 4 - taps), (0, 0))).reshape(48, 64)


def exchange_sum(value, axes, order=None):
    peers = lax.axis_size(axes)
    copies = jnp.broadcast_to(value[None], (peers,) + value.shape)
    groups = None if order is None else [order]
    return jnp.sum(lax.all_to_all(copies, axes, 0, 0, axis_index_groups=groups).astype(F32), axis=0)


def shards(fake, real, vgg_first, vgg_second, lpips_weights, critic_conv, critic_head):
    count = lax.axis_size(ROWS)
    first_row = (lax.axis_index(ROWS) * 4).astype(jnp.int32)[None]
    images = jnp.concatenate([fake, real], axis=0)
    far_pairs = [(k, k + 1) for k in range(15, count - 1, 16)]
    whole = images.astype(F32)
    under = lax.ppermute(whole, ROWS, [(b, b + MIDDLE) for a, b in far_pairs])
    upper = lax.ppermute(whole, ROWS, [(a, b + MIDDLE) for a, b in far_pairs])
    critic_rows = weight_rows(critic_conv)
    spread, critic_fwd, head = critic_weights(critic_rows, critic_head[None])
    previous = lax.ppermute(images, ROWS, [(k, k + 1) for k in range(count - 1) if k % 16 < 15])
    following = lax.ppermute(whole, ROWS, [(k + 1, k) for k in range(count - 1) if k % 16 < 15])
    early = lax.ppermute(upper, ("zh",) + ROWS, [(b + MIDDLE, b) for a, b in far_pairs])
    rest = [(count + a, count + b) for a, b in far_pairs]
    for base in (0, count):
        rest += [(base + b + MIDDLE, base + a) for a, b in far_pairs]
    sums = critic(first_row, under, upper, previous, images, spread, critic_fwd, head)
    plane = exchange_sum(sums.astype(jnp.float16), PLANE, PLANE_ORDER)
    plane, first, second, again = lax.optimization_barrier(
        (plane, weight_rows(vgg_first), jnp.transpose(vgg_second, (2, 3, 0, 1)), critic_rows)
    )
    *weights, copied = feature_weights(first_row, first, second, again, following, early, under, images)
    late = lax.ppermute(copied, ("zh",) + ROWS, rest)
    total = exchange_sum((plane * (1.0 / 32.0)).astype(jnp.float16), COLUMN, COLUMN_ORDER)
    grad_image = features(
        first_row, *weights, previous, images, following, early, late, lpips_weights[:, None], spread, critic_fwd, head
    )
    conv_grad, head_grad = finish(total)
    return grad_image[None], jnp.transpose(conv_grad, (3, 0, 1, 2)), head_grad[0]


def solution(mesh):
    wide = Mesh(mesh.devices.reshape(2, 4, 4, 8, 2), ("zh", "y", "x", "zl", "c"))
    return jax.shard_map(
        shards,
        mesh=wide,
        in_specs=(P(DP, None, ROWS, None), P(DP, None, ROWS, None), P(), P(), P(), P(), P()),
        out_specs=(P(DP, None, ROWS, None), P(), P()),
        check_vma=False,
    )
```
